256 devices in a mesh: rep: 64 (over z, y, core), mdl: 4 (over x).
Axes of the slice: x: 4, y: 4, z: 8, core: 2. Of those that a mesh axis runs over, the one named last changes fastest.
Arguments:
- grads: bfloat16 [64, 512, 128, 128], P('rep', 'mdl'), may hold values from -3600 to 3600
- momentum: bfloat16 [64, 512, 128, 128], P('rep', 'mdl'), may hold values from -6 to 6
- weight: bfloat16 [512, 128, 128], P('mdl'), may hold values from -6 to 6
- select: int32 [512, 4], P('mdl'), may hold values from 0 to 63, all different within a row
Outputs:
- new_weight: bfloat16 [512, 128, 128], P('mdl')
- new_momentum: bfloat16 [64, 512, 128, 128], P('rep', 'mdl')
The draws below stay inside these ranges and needn't reach their ends.
Inputs may be any that keep to these rules, and one draw needn't show every extreme that they name: `select`: each row names 4 different blocks.
All inputs are finite; a program needn't handle non-finite values.
Results may differ from the reference program's by a relative error of at most 0.001.
Values may be sent and summed in bfloat16 or wider, within the bound.
No kernel may reach another device: no remote copies, remote signals or barrier semaphores. Data moves between devices by JAX's collectives and lax.ppermute only.
A program may use at most 128 MiB of HBM per device.

```python
import math
import jax
import jax.numpy as jnp
from jax import lax

GROUP = 128
FB = 16
KSEL = 4
NBS = 8
NBLK = 64
GROUPS = 512
REPS = 64


def draw_grads(key, part):
    key = jax.random.fold_in(key, 11)
    keys = jax.random.split(key, 4)
    shape = (REPS, GROUPS, GROUP, GROUP)
    base = jnp.clip(jax.random.normal(keys[0], shape, jnp.float32), -4.0, 4.0)
    row_scale = jnp.exp(jax.random.uniform(keys[1], (REPS, GROUPS, GROUP, 1), jnp.float32, 0.0, math.log(10.0)))
    col_scale = jnp.exp(jax.random.uniform(keys[2], (1, 1, 1, GROUP), jnp.float32, 0.0, math.log(10.0)))
    position = jnp.arange(GROUPS, dtype=jnp.float32)
    ramp = jnp.sqrt(1.0 + 4.0 * position / max(GROUPS - 1, 1)).reshape(1, GROUPS, 1, 1)
    spike_at = jax.random.randint(keys[3], (REPS,), 0, GROUPS)
    spike = jnp.where(jnp.arange(GROUPS, dtype=jnp.int32)[None, :] == spike_at[:, None], 4.0, 1.0)
    values = base * row_scale * col_scale * ramp * spike[:, :, None, None]
    return values.astype(jnp.bfloat16)


def block_scale(stream_key, dims, shards, low, high):
    factor_of, own = 1.0, jax.random.fold_in(stream_key, 6)
    for axis_at, blocks in shards:
        heights = jnp.exp(jax.random.uniform(jax.random.fold_in(own, axis_at), (blocks,), jnp.float32, low / len(shards), high / len(shards)))
        factor_of = factor_of * jnp.repeat(heights, dims[axis_at] // blocks).reshape([-1 if axis == axis_at else 1 for axis in range(len(dims))])
    return factor_of


def choose_distinct(own_key, rows, count, top, lift):
    ranking = jax.random.permutation(jax.random.fold_in(own_key, 1), count)
    boost = ranking
    for power in range(3):
        boost = boost * boost // count
    boost = boost * lift // count
    chance = jax.random.randint(jax.random.fold_in(own_key, 2), (rows, count), 0, 4096) + boost
    sure = jax.random.permutation(jax.random.fold_in(own_key, 3), rows)[jnp.arange(count) % rows]
    chance = jnp.where(jnp.arange(rows)[:, None] == sure[None, :], 1 << 14, chance)
    score = chance * count + jnp.arange(count)
    return lax.top_k(score.astype(jnp.int32), top)[1].astype(jnp.int32)


def noise(key, shape, scale, limit, cuts=(), kind=jnp.bfloat16):
    result = jax.random.normal(key, shape, jnp.float32) * scale
    if len(cuts) > 0:
        result = block_scale(key, shape, cuts, -0.22, 0.18) * result
    return jnp.clip(result, min=-limit, max=limit).astype(kind)


def setup_inputs(seed: int = 0) -> dict:
    key_list = jax.random.split(jax.random.key(seed), 5)
    return {
        "grads": draw_grads(jax.random.fold_in(key_list[4], 71), 0),
        "momentum": noise(key_list[1], (REPS, GROUPS, GROUP, GROUP), 1.0, 6.0, ((0, 64), (1, 4))),
        "weight": noise(key_list[2], (GROUPS, GROUP, GROUP), 1.0, 6.0, ((0, 4),)),
        "select": choose_distinct(key_list[3], GROUPS, NBLK, KSEL, 0),
    }


momentum_retention = 0.9
learn_rate = 0.1
eps = 1e-06

def dct_matrix(length):
    freq = jnp.arange(length, dtype=jnp.float32)[:, None]
    sample = jnp.arange(length, dtype=jnp.float32)[None, :]
    factor = jnp.where(freq == 0, jnp.sqrt(1.0 / length), jnp.sqrt(2.0 / length))
    return factor * jnp.cos(jnp.pi * (2.0 * sample + 1.0) * freq / (2.0 * length))

def to_blocks(groups):
    total = groups.shape[0]
    return groups.reshape(total, NBS, FB, NBS, FB).transpose(0, 1, 3, 2, 4).reshape(total, NBLK, FB * FB)

def from_blocks(block_tiles):
    total = block_tiles.shape[0]
    return block_tiles.reshape(total, NBS, NBS, FB, FB).transpose(0, 1, 3, 2, 4).reshape(total, GROUP, GROUP)

def forward_cosine(transform, groups):
    left = jnp.einsum('kn,cnm->ckm', transform, groups, precision=lax.Precision.HIGHEST)
    return jnp.einsum('ckm,lm->ckl', left, transform, precision=lax.Precision.HIGHEST)

def inverse(transform, spectrum):
    left = jnp.einsum('kn,ckl->cnl', transform, spectrum, precision=lax.Precision.HIGHEST)
    return jnp.einsum('cnl,lm->cnm', left, transform, precision=lax.Precision.HIGHEST)

def decode(transform, grand_totals, select, weight):
    indicator_matrix = (select[:, :, None] == jnp.arange(NBLK, dtype=jnp.int32)[None, None, :]).astype(jnp.float32)
    complete_spectrum = jnp.einsum('dwk,dwh->dkh', indicator_matrix, grand_totals, precision=lax.Precision.HIGHEST)
    decoded = inverse(transform, from_blocks(complete_spectrum))
    inv_rms = lax.rsqrt(lax.optimization_barrier(jnp.mean(decoded * decoded, axis=(1, 2), keepdims=True)) + eps)
    return (weight.astype(jnp.float32) - learn_rate * decoded * inv_rms).astype(jnp.bfloat16)

def reference(grads, momentum, weight, select):
    transform = dct_matrix(GROUP)
    entry_count = float(GROUPS * GROUP * GROUP)
    retain = 1.0 - jnp.any(select[:, :, None] == jnp.arange(NBLK, dtype=jnp.int32)[None, None, :], axis=1).astype(jnp.float32)

    def replica(carry, pieces):
        grad_one, moment_one = pieces
        grad_wide = grad_one.astype(jnp.float32)
        square_sum = jnp.sum(grad_wide * grad_wide)
        clip = jnp.minimum(1.0, lax.rsqrt(square_sum / entry_count))
        moment = momentum_retention * moment_one.astype(jnp.float32) + clip * grad_wide
        block_tiles = to_blocks(forward_cosine(transform, moment))
        coeffs = jnp.take_along_axis(block_tiles, select[:, :, None], axis=1)
        residual = from_blocks(block_tiles * retain[:, :, None])
        latest_moment = inverse(transform, residual).astype(jnp.bfloat16)
        return (carry + coeffs, latest_moment)
    start = jnp.zeros((GROUPS, KSEL, FB * FB), jnp.float32)
    grand_totals, new_momentum = lax.scan(replica, start, (grads, momentum))
    new_weight = decode(transform, grand_totals, select, weight)
    return (new_weight, new_momentum)
```

```python
import functools

import jax
import jax.numpy as jnp
import ml_dtypes
import numpy as np
from jax import lax
from jax.experimental import pallas as pl
from jax.experimental.pallas import tpu as pltpu
from jax.sharding import PartitionSpec as P

GROUP = 128
FB = 16
NBS = 8
KSEL = 4
REPS = 64
CHIPS = 32
PAIRS = 64
HALF = 32
momentum_retention = 0.9
learn_rate = 0.1
eps = 1e-06


def dct_tables():
    freq = np.arange(GROUP, dtype=np.float64)[:, None]
    sample = np.arange(GROUP, dtype=np.float64)[None, :]
    factor = np.where(freq == 0, np.sqrt(1.0 / GROUP), np.sqrt(2.0 / GROUP))
    full = factor * np.cos(np.pi * (2.0 * sample + 1.0) * freq / (2.0 * GROUP))
    high = full.astype(ml_dtypes.bfloat16)
    low = (full - high.astype(np.float64)).astype(ml_dtypes.bfloat16)
    return high, low


def split(wide):
    high = wide.astype(jnp.bfloat16)
    low = (wide - high.astype(jnp.float32)).astype(jnp.bfloat16)
    return high, low


def dot(a, b, dims=(((1,), (0,)), ((), ()))):
    return lax.dot_general(a, b, dims, preferred_element_type=jnp.float32)


NT = (((1,), (1,)), ((), ()))
TN = (((0,), (0,)), ((), ()))


def gather_rows(table, blocks):
    return jnp.concatenate(
        [table[pl.ds(pl.multiple_of(b * FB, FB), FB), :] for b in blocks], axis=0
    )


def blocks_of(sel, pair):
    picked = [sel[pair * 8 + q] for q in range(8)]
    return [b // NBS for b in picked], [b % NBS for b in picked]


def square_kernel(g, out):
    @pl.when(pl.program_id(0) == 0)
    def _():
        out[...] = jnp.zeros_like(out)

    wide = g[...].astype(jnp.float32)
    wide = (wide * wide).reshape(-1, 8, GROUP)
    out[...] += jnp.sum(wide, axis=0)


def square_sums(grads):
    step = 16
    groups = grads.shape[0]
    return pl.pallas_call(
        square_kernel,
        grid=(groups // step,),
        in_specs=[pl.BlockSpec((step, GROUP, GROUP), lambda i: (i, 0, 0))],
        out_specs=pl.BlockSpec((8, GROUP), lambda i: (0, 0)),
        out_shape=jax.ShapeDtypeStruct((8, GROUP), jnp.float32),
        cost_estimate=pl.CostEstimate(flops=4 << 20, bytes_accessed=4 << 20, transcendentals=0),
        name="square_sums",
    )(grads)


def forward_kernel(step, sel, off, g, m, t_high, t_low, cg, cm):
    lane = lax.broadcasted_iota(jnp.int32, (FB, GROUP), 1) // FB
    base = (off[0] + pl.program_id(0)) * step
    for p in range(step):
        rows, cols = blocks_of(sel, base + p)
        row_high, row_low = gather_rows(t_high, rows), gather_rows(t_low, rows)
        col_high, col_low = gather_rows(t_high, cols), gather_rows(t_low, cols)
        picked = []
        for s in range(2):
            both = jnp.concatenate([g[2 * p + s], m[2 * p + s]], axis=1)
            own = slice(64 * s, 64 * s + 64)
            left = jnp.concatenate([row_high[own], row_low[own]], axis=0)
            prod = dot(left, both)
            picked.append(prod[:64] + prod[64:])
        left = jnp.concatenate(picked, axis=0)
        left = jnp.concatenate([left[:, :GROUP], left[:, GROUP:]], axis=0)
        high, low = split(left)
        lhs = jnp.concatenate([high, low], axis=1)
        rhs = jnp.concatenate(
            [
                jnp.concatenate([col_high, col_high], axis=1),
                jnp.concatenate([col_low, jnp.zeros_like(col_low)], axis=1),
            ],
            axis=0,
        )
        prod = dot(lhs, rhs, NT)
        prod = prod[:, :GROUP] + prod[:, GROUP:]
        for at, ref in ((0, cg), (GROUP, cm)):
            tile = prod[at : at + FB]
            for q in range(1, 8):
                tile = jnp.where(lane == q, prod[at + FB * q : at + FB * q + FB], tile)
            ref[p] = tile


def forward(sel, half, grads, momentum, t_high, t_low):
    step = 4
    table = pl.BlockSpec((GROUP, GROUP), lambda i, sel, off: (0, 0))
    groups = pl.BlockSpec((2 * step, GROUP, GROUP), lambda i, sel, off: (off[0] + i, 0, 0))
    tiles = pl.BlockSpec((step, FB, GROUP), lambda i, sel, off: (i, 0, 0))
    shape = jax.ShapeDtypeStruct((HALF, FB, GROUP), jnp.float32)
    return pl.pallas_call(
        functools.partial(forward_kernel, step),
        grid_spec=pltpu.PrefetchScalarGridSpec(
            num_scalar_prefetch=2,
            grid=(HALF // step,),
            in_specs=[groups, groups, table, table],
            out_specs=[tiles, tiles],
        ),
        out_shape=[shape, shape],
        cost_estimate=pl.CostEstimate(flops=2 << 30, bytes_accessed=5 << 20, transcendentals=0),
        name="forward_cosine",
    )(sel, half * (HALF // step), grads, momentum, t_high, t_low)


def decode_pair(coeffs, rows, cols, t_high, t_low):
    lane = lax.broadcasted_iota(jnp.int32, (FB, GROUP), 1) // FB
    row_high, row_low = gather_rows(t_high, rows), gather_rows(t_low, rows)
    col_high, col_low = gather_rows(t_high, cols), gather_rows(t_low, cols)
    none = jnp.zeros((FB, GROUP), jnp.float32)
    parts = jnp.concatenate([jnp.where(lane == q, coeffs, none) for q in range(8)], axis=0)
    high, low = split(parts)
    lhs = jnp.concatenate([high, low], axis=1)
    rhs = jnp.concatenate(
        [
            jnp.concatenate([col_high, col_low], axis=1),
            jnp.concatenate([col_high, jnp.zeros_like(col_low)], axis=1),
        ],
        axis=0,
    )
    prod = dot(lhs, rhs)
    high, low = split(prod[:, :GROUP] + prod[:, GROUP:])
    result = []
    for s in range(2):
        own = slice(64 * s, 64 * s + 64)
        left = jnp.concatenate([row_high[own], row_high[own], row_low[own]], axis=0)
        right = jnp.concatenate([high[own], low[own], high[own]], axis=0)
        result.append(dot(left, right, TN))
    return result


def momentum_kernel(step, sel, off, clip, g, m, coeffs, t_high, t_low, _, out):
    base = (off[0] + pl.program_id(0)) * step
    for p in range(step):
        rows, cols = blocks_of(sel, base + p)
        for s, taken in enumerate(decode_pair(coeffs[p], rows, cols, t_high, t_low)):
            wide = momentum_retention * m[2 * p + s].astype(jnp.float32)
            wide += clip[0] * g[2 * p + s].astype(jnp.float32)
            out[2 * p + s] = (wide - taken).astype(jnp.bfloat16)


def weight_kernel(step, sel, off, w, coeffs, t_high, t_low, _, out):
    base = (off[0] + pl.program_id(0)) * step
    for p in range(step):
        rows, cols = blocks_of(sel, base + p)
        for s, taken in enumerate(decode_pair(coeffs[p], rows, cols, t_high, t_low)):
            wide = w[2 * p + s].astype(jnp.float32) - taken
            out[2 * p + s] = wide.astype(jnp.bfloat16)


def decode_half(kernel, scalars, half, arrays, coeffs, t_high, t_low, before, name):
    step = 4
    table = pl.BlockSpec((GROUP, GROUP), lambda i, sel, off, *_: (0, 0))
    groups = pl.BlockSpec((2 * step, GROUP, GROUP), lambda i, sel, off, *_: (off[0] + i, 0, 0))
    tiles = pl.BlockSpec((step, FB, GROUP), lambda i, *_: (i, 0, 0))
    scalars = (scalars[0], half * (HALF // step), *scalars[1:])
    operands = (*scalars, *arrays, coeffs, t_high, t_low)
    specs = [groups] * len(arrays) + [tiles, table, table]
    if before is None:
        inner = kernel
        kernel = lambda *refs: inner(*refs[:-1], None, refs[-1])
        aliases = {}
    else:
        aliases = {len(operands): 0}
        operands += (before,)
        specs.append(pl.BlockSpec(memory_space=pl.ANY))
    return pl.pallas_call(
        kernel,
        grid_spec=pltpu.PrefetchScalarGridSpec(
            num_scalar_prefetch=len(scalars),
            grid=(HALF // step,),
            in_specs=specs,
            out_specs=groups,
        ),
        out_shape=jax.ShapeDtypeStruct((2 * PAIRS, GROUP, GROUP), jnp.bfloat16),
        input_output_aliases=aliases,
        cost_estimate=pl.CostEstimate(flops=2 << 30, bytes_accessed=(2 << 20) * (1 + len(arrays)), transcendentals=0),
        name=name,
    )(*operands)


def total_kernel(parts, out):
    total = jnp.sum(parts[...], axis=0)
    lane = lax.broadcasted_iota(jnp.int32, (FB, GROUP), 1)
    square = total * total
    first = jnp.sum(jnp.where(lane < 64, square, 0.0))
    second = jnp.sum(jnp.where(lane < 64, 0.0, square))
    mean = jnp.where(lane < 64, first, second) / (GROUP * GROUP)
    out[...] = jnp.broadcast_to(learn_rate * total * lax.rsqrt(mean + eps), out.shape)


def scaled_totals(parts):
    return pl.pallas_call(
        total_kernel,
        out_shape=jax.ShapeDtypeStruct((CHIPS, FB, GROUP), jnp.float32),
        name="scaled_totals",
    )(parts)


def per_device(grads, momentum, weight, select):
    t_high, t_low = (jnp.asarray(table) for table in dct_tables())
    grads, momentum = grads[0], momentum[0]
    sel = select.reshape(-1)
    own = lax.rem(lax.axis_index("rep"), 2).astype(jnp.int32).reshape(1)
    other = 1 - own
    same_core = [list(range(c, REPS, 2)) for c in range(2)]
    swap_core = [(i, i ^ 1) for i in range(REPS)]
    swap = lambda x: lax.ppermute(x, "rep", swap_core)
    exchange = lambda x: lax.all_to_all(x, "rep", 0, 0, tiled=True, axis_index_groups=same_core)

    sums = square_sums(grads)
    square_sum = jnp.sum(sums).reshape(1, 1)
    square_sum += lax.ppermute(square_sum, "mdl", [(i, i ^ 1) for i in range(4)])
    square_sum += lax.ppermute(square_sum, "mdl", [(i, i ^ 2) for i in range(4)])
    entry_count = float(4 * grads.size)
    clip = jnp.minimum(1.0, lax.rsqrt(square_sum / entry_count))

    g_other, m_other = forward(sel, other, grads, momentum, t_high, t_low)
    g_own, m_own = forward(sel, own, grads, momentum, t_high, t_low)
    c_other = momentum_retention * m_other + clip[0, 0] * g_other
    c_own = momentum_retention * m_own + clip[0, 0] * g_own
    parts = exchange(c_own + swap(c_other))
    clip = clip.reshape(1)
    new_momentum = decode_half(
        functools.partial(momentum_kernel, 4), (sel, clip), other, (grads, momentum),
        c_other, t_high, t_low, None, "momentum_other",
    )
    mine = scaled_totals(parts)
    totals_own = exchange(mine)
    new_momentum = decode_half(
        functools.partial(momentum_kernel, 4), (sel, clip), own, (grads, momentum),
        c_own, t_high, t_low, new_momentum, "momentum_own",
    )
    totals_other = swap(totals_own)
    new_weight = decode_half(
        functools.partial(weight_kernel, 4), (sel,), own, (weight,),
        totals_own, t_high, t_low, None, "weight_own",
    )
    new_weight = decode_half(
        functools.partial(weight_kernel, 4), (sel,), other, (weight,),
        totals_other, t_high, t_low, new_weight, "weight_other",
    )
    return (new_weight, new_momentum[None])


def solution(mesh):
    return jax.shard_map(
        per_device,
        mesh=mesh,
        in_specs=(
            P("rep", "mdl", None, None),
            P("rep", "mdl", None, None),
            P("mdl", None, None),
            P("mdl", None),
        ),
        out_specs=(P("mdl", None, None), P("rep", "mdl", None, None)),
        check_vma=False,
    )
```

```python
import functools

import jax
import jax.numpy as jnp
import ml_dtypes
import numpy as np
from jax import lax
from jax.experimental import pallas as pl
from jax.experimental.pallas import tpu as pltpu
from jax.sharding import PartitionSpec as P

GROUP = 128
FB = 16
NBS = 8
KSEL = 4
REPS = 64
CHIPS = 32
PAIRS = 64
HALF = 32
momentum_retention = 0.9
learn_rate = 0.1
eps = 1e-06


def dct_tables():
    freq = np.arange(GROUP, dtype=np.float64)[:, None]
    sample = np.arange(GROUP, dtype=np.float64)[None, :]
    factor = np.where(freq == 0, np.sqrt(1.0 / GROUP), np.sqrt(2.0 / GROUP))
    full = factor * np.cos(np.pi * (2.0 * sample + 1.0) * freq / (2.0 * GROUP))
    high = full.astype(ml_dtypes.bfloat16)
    low = (full - high.astype(np.float64)).astype(ml_dtypes.bfloat16)
    return high, low


def split(wide):
    high = wide.astype(jnp.bfloat16)
    low = (wide - high.astype(jnp.float32)).astype(jnp.bfloat16)
    return high, low


def dot(a, b, dims=(((1,), (0,)), ((), ()))):
    return lax.dot_general(a, b, dims, preferred_element_type=jnp.float32)


NT = (((1,), (1,)), ((), ()))
TN = (((0,), (0,)), ((), ()))


def gather_rows(table, blocks):
    return jnp.concatenate(
        [table[pl.ds(pl.multiple_of(b * FB, FB), FB), :] for b in blocks], axis=0
    )


def blocks_of(sel, pair):
    picked = [sel[pair * 8 + q] for q in range(8)]
    return [b // NBS for b in picked], [b % NBS for b in picked]


ANY = pl.BlockSpec(memory_space=pl.ANY)
VMEM = pl.BlockSpec(memory_space=pltpu.VMEM)
SMEM = pl.BlockSpec(memory_space=pltpu.SMEM)
STEP = 8
CHUNKS = HALF // STEP
CHUNK_GROUPS = 2 * STEP


def square_kernel(g, out, buf, sem):
    chunks = sem.shape[0]
    size = g.shape[0] // chunks

    def load(c):
        part = pl.ds(c * size, size)
        return pltpu.make_async_copy(g.at[part], buf.at[part], sem.at[c])

    for c in range(chunks):
        load(c).start()

    def body(c, total):
        load(c).wait()
        wide = buf[pl.ds(c * size, size)].astype(jnp.float32)
        return total + jnp.sum((wide * wide).reshape(-1, 64, GROUP), axis=0)

    total = lax.fori_loop(0, chunks, body, jnp.zeros((64, GROUP), jnp.float32))
    out[...] = jnp.sum(total.reshape(8, 8, GROUP), axis=0)


def square_sums(grads):
    return pl.pallas_call(
        square_kernel,
        in_specs=[ANY],
        out_specs=VMEM,
        out_shape=jax.ShapeDtypeStruct((8, GROUP), jnp.float32),
        scratch_shapes=[pltpu.VMEM(grads.shape, grads.dtype), pltpu.SemaphoreType.DMA((8,))],
        compiler_params=pltpu.CompilerParams(vmem_limit_bytes=51 << 20),
        cost_estimate=pl.CostEstimate(flops=4 << 20, bytes_accessed=4 << 20, transcendentals=0),
        name="square_sums",
    )(grads)


def load_half(arrays, bufs, sem, base):
    def load(a, c):
        return pltpu.make_async_copy(
            arrays[a].at[pl.ds(2 * base + c * CHUNK_GROUPS, CHUNK_GROUPS)],
            bufs[a].at[pl.ds(c * CHUNK_GROUPS, CHUNK_GROUPS)],
            sem.at[a, c],
        )

    for c in range(CHUNKS):
        for a in range(len(arrays)):
            load(a, c).start()

    def wait(c):
        for a in range(len(arrays)):
            load(a, c).wait()

    return wait


def forward_pair(g, m, rows, cols, t_high, t_low):
    lane = lax.broadcasted_iota(jnp.int32, (FB, GROUP), 1) // FB
    row_high, row_low = gather_rows(t_high, rows), gather_rows(t_low, rows)
    col_high, col_low = gather_rows(t_high, cols), gather_rows(t_low, cols)
    picked = []
    for s in range(2):
        own = slice(64 * s, 64 * s + 64)
        left = jnp.concatenate([row_high[own], row_low[own]], axis=0)
        prod = dot(left, jnp.concatenate([g[s], m[s]], axis=1))
        picked.append(prod[:64] + prod[64:])
    left = jnp.concatenate(picked, axis=0)
    left = jnp.concatenate([left[:, :GROUP], left[:, GROUP:]], axis=0)
    high, low = split(left)
    lhs = jnp.concatenate([high, low], axis=1)
    rhs = jnp.concatenate(
        [
            jnp.concatenate([col_high, col_high], axis=1),
            jnp.concatenate([col_low, jnp.zeros_like(col_low)], axis=1),
        ],
        axis=0,
    )
    prod = dot(lhs, rhs, NT)
    tiles = []
    for at in (0, GROUP):
        tile = None
        for q in range(8):
            part = prod[at + FB * q : at + FB * q + FB]
            part = part[:, :GROUP] + part[:, GROUP:]
            tile = part if q == 0 else jnp.where(lane == q, part, tile)
        tiles.append(tile)
    return tiles


def forward_kernel(sel, off, g, m, t_high, t_low, cg, cm, g_buf, m_buf, sem):
    base = off[0] * HALF
    wait = load_half((g, m), (g_buf, m_buf), sem, base)

    def body(c, _):
        wait(c)
        for u in range(STEP):
            p = c * STEP + u
            rows, cols = blocks_of(sel, base + p)
            pair = pl.ds(2 * p, 2)
            cg[p], cm[p] = forward_pair(g_buf[pair], m_buf[pair], rows, cols, t_high, t_low)
        return 0

    lax.fori_loop(0, CHUNKS, body, 0)


def forward(sel, half, grads, momentum, t_high, t_low):
    shape = jax.ShapeDtypeStruct((HALF, FB, GROUP), jnp.float32)
    buf = pltpu.VMEM((2 * HALF, GROUP, GROUP), jnp.bfloat16)
    return pl.pallas_call(
        forward_kernel,
        in_specs=[SMEM, SMEM, ANY, ANY, VMEM, VMEM],
        out_specs=[VMEM, VMEM],
        out_shape=[shape, shape],
        scratch_shapes=[buf, buf, pltpu.SemaphoreType.DMA((2, CHUNKS))],
        compiler_params=pltpu.CompilerParams(vmem_limit_bytes=51 << 20),
        cost_estimate=pl.CostEstimate(flops=2 << 30, bytes_accessed=5 << 20, transcendentals=0),
        name="forward_cosine",
    )(sel, half, grads, momentum, t_high, t_low)


def clip_of(first, second):
    square_sum = jnp.sum(first + second)
    entry_count = float(4 * 2 * PAIRS * GROUP * GROUP)
    return jnp.minimum(1.0, lax.rsqrt(jnp.full((1, GROUP), square_sum) / entry_count))


def combine_kernel(first, second, g_other, m_other, g_own, m_own, c_other, c_own, clip):
    clip[...] = clip_of(first[...], second[...])
    scale = clip[...].reshape(1, 1, GROUP)
    c_other[...] = momentum_retention * m_other[...] + scale * g_other[...]
    c_own[...] = momentum_retention * m_own[...] + scale * g_own[...]


def combine(first, second, *tiles):
    shape = jax.ShapeDtypeStruct((HALF, FB, GROUP), jnp.float32)
    return pl.pallas_call(
        combine_kernel,
        in_specs=[VMEM] * 6,
        out_specs=[VMEM] * 3,
        out_shape=[shape, shape, jax.ShapeDtypeStruct((1, GROUP), jnp.float32)],
        input_output_aliases={2: 0, 4: 1},
        compiler_params=pltpu.CompilerParams(vmem_limit_bytes=8 << 20),
        cost_estimate=pl.CostEstimate(flops=1 << 20, bytes_accessed=1 << 20, transcendentals=0),
        name="combine",
    )(first, second, *tiles)


def decode_pair(coeffs, rows, cols, t_high, t_low, t_left):
    lane = lax.broadcasted_iota(jnp.int32, (FB, GROUP), 1) // FB
    row_of = jnp.zeros((FB, GROUP), jnp.int32)
    for q in range(8):
        row_of = jnp.where(lane == q, rows[q], row_of)
    parts = jnp.concatenate([jnp.where(row_of == b, coeffs, 0.0) for b in range(NBS)], axis=0)
    high, low = split(parts)
    left = dot(t_left[...], jnp.concatenate([high, low, high], axis=0))
    high, low = split(left)
    none = jnp.zeros((64, GROUP), jnp.bfloat16)

    def both(table):
        chosen = gather_rows(table, cols)
        return jnp.concatenate(
            [
                jnp.concatenate([chosen[:64], none], axis=1),
                jnp.concatenate([none, chosen[64:]], axis=1),
            ],
            axis=0,
        )

    col_high, col_low = both(t_high), both(t_low)
    result = dot(
        jnp.concatenate([high, low, high], axis=1),
        jnp.concatenate([col_high, col_high, col_low], axis=0),
    )
    return result[:, :GROUP], result[:, GROUP:]


def decode_kernel(count, sel, off, *refs):
    arrays, refs = refs[:count], refs[count:]
    scale, coeffs, t_high, t_low, t_left = refs[:5]
    out = refs[-(count + 4)]
    bufs = refs[-(count + 3) : -3]
    out_buf, sem, out_sem = refs[-3:]
    base = off[0] * HALF
    wait = load_half(arrays, bufs, sem, base)

    def store(c):
        return pltpu.make_async_copy(
            out_buf.at[pl.ds(c * CHUNK_GROUPS, CHUNK_GROUPS)],
            out.at[pl.ds(2 * base + c * CHUNK_GROUPS, CHUNK_GROUPS)],
            out_sem.at[c],
        )

    def body(c, _):
        wait(c)
        for u in range(STEP):
            p = c * STEP + u
            rows, cols = blocks_of(sel, base + p)
            for s, taken in enumerate(decode_pair(coeffs[p], rows, cols, t_high, t_low, t_left)):
                wide = bufs[0][2 * p + s].astype(jnp.float32)
                if count == 2:
                    wide = momentum_retention * bufs[1][2 * p + s].astype(jnp.float32) + scale[...] * wide
                out_buf[2 * p + s] = (wide - taken).astype(jnp.bfloat16)
        store(c).start()
        return 0

    lax.fori_loop(0, CHUNKS, body, 0)
    for c in range(CHUNKS):
        store(c).wait()


def decode_half(sel, half, arrays, scale, coeffs, tables, before, name):
    operands = (sel, half, *arrays, scale, coeffs, *tables)
    specs = [SMEM, SMEM] + [ANY] * len(arrays) + [VMEM] * 5
    aliases = {}
    if before is not None:
        aliases = {len(operands): 0}
        operands += (before,)
        specs.append(ANY)
    buf = pltpu.VMEM((2 * HALF, GROUP, GROUP), jnp.bfloat16)
    return pl.pallas_call(
        functools.partial(decode_kernel, len(arrays)),
        in_specs=specs,
        out_specs=ANY,
        out_shape=jax.ShapeDtypeStruct((2 * PAIRS, GROUP, GROUP), jnp.bfloat16),
        scratch_shapes=[buf] * (len(arrays) + 1)
        + [pltpu.SemaphoreType.DMA((len(arrays), CHUNKS)), pltpu.SemaphoreType.DMA((CHUNKS,))],
        input_output_aliases=aliases,
        compiler_params=pltpu.CompilerParams(vmem_limit_bytes=51 << 20),
        cost_estimate=pl.CostEstimate(flops=2 << 30, bytes_accessed=(2 << 20) * (1 + len(arrays)), transcendentals=0),
        name=name,
    )(*operands)


def total_kernel(parts, out):
    total = jnp.sum(parts[...], axis=0)
    lane = lax.broadcasted_iota(jnp.int32, (FB, GROUP), 1)
    square = total * total
    first = jnp.sum(jnp.where(lane < 64, square, 0.0))
    second = jnp.sum(jnp.where(lane < 64, 0.0, square))
    mean = jnp.where(lane < 64, first, second) / (GROUP * GROUP)
    out[...] = jnp.broadcast_to(learn_rate * total * lax.rsqrt(mean + eps), out.shape)


def scaled_totals(parts):
    return pl.pallas_call(
        total_kernel,
        in_specs=[VMEM],
        out_specs=VMEM,
        out_shape=jax.ShapeDtypeStruct((CHIPS, FB, GROUP), jnp.float32),
        compiler_params=pltpu.CompilerParams(vmem_limit_bytes=8 << 20),
        cost_estimate=pl.CostEstimate(flops=1 << 20, bytes_accessed=1 << 19, transcendentals=0),
        name="scaled_totals",
    )(parts)


def per_device(grads, momentum, weight, select):
    high, low = dct_tables()
    left = np.concatenate([high.T, high.T, low.T], axis=1)
    t_high, t_low, t_left = tables = tuple(jnp.asarray(table) for table in (high, low, left))
    grads, momentum = grads[0], momentum[0]
    sel = select.reshape(-1)
    own = lax.rem(lax.axis_index("rep"), 2).astype(jnp.int32).reshape(1)
    other = 1 - own
    same_core = [list(range(c, REPS, 2)) for c in range(2)]
    swap_core = [(i, i ^ 1) for i in range(REPS)]
    swap = lambda x: lax.ppermute(x, "rep", swap_core)
    exchange = lambda x: lax.all_to_all(x, "rep", 0, 0, tiled=True, axis_index_groups=same_core)

    sums = square_sums(grads)
    sums += lax.ppermute(sums, "mdl", [(i, i ^ 1) for i in range(4)])
    g_other, m_other = forward(sel, other, grads, momentum, t_high, t_low)
    sums, g_other, m_other = lax.optimization_barrier((sums, g_other, m_other))
    far = lax.ppermute(sums, "mdl", [(i, i ^ 2) for i in range(4)])
    g_own, m_own = forward(sel, own, grads, momentum, t_high, t_low)
    c_other, c_own, clip = combine(sums, far, g_other, m_other, g_own, m_own)
    chip, c_other, c_own = lax.optimization_barrier((c_own + swap(c_other), c_other, c_own))
    parts = exchange(chip)
    new_momentum = decode_half(
        sel, other, (grads, momentum), clip, c_other, tables, None, "momentum_other"
    )
    parts, new_momentum = lax.optimization_barrier((parts, new_momentum))
    mine, c_own = lax.optimization_barrier((scaled_totals(parts), c_own))
    totals_own = exchange(mine)
    new_momentum = decode_half(
        sel, own, (grads, momentum), clip, c_own, tables, new_momentum, "momentum_own"
    )
    totals_own, new_momentum = lax.optimization_barrier((totals_own, new_momentum))
    totals_other = swap(totals_own)
    new_weight = decode_half(sel, own, (weight,), clip, totals_own, tables, None, "weight_own")
    new_weight = decode_half(
        sel, other, (weight,), clip, totals_other, tables, new_weight, "weight_other"
    )
    return (new_weight, new_momentum[None])


def solution(mesh):
    return jax.shard_map(
        per_device,
        mesh=mesh,
        in_specs=(
            P("rep", "mdl", None, None),
            P("rep", "mdl", None, None),
            P("mdl", None, None),
            P("mdl", None),
        ),
        out_specs=(P("mdl", None, None), P("rep", "mdl", None, None)),
        check_vma=False,
    )
```

```python
import functools

import jax
import jax.numpy as jnp
import ml_dtypes
import numpy as np
from jax import lax
from jax.experimental import pallas as pl
from jax.experimental.pallas import tpu as pltpu
from jax.sharding import PartitionSpec as P

GROUP = 128
FB = 16
NBS = 8
KSEL = 4
REPS = 64
CHIPS = 32
PAIRS = 64
HALF = 32
momentum_retention = 0.9
learn_rate = 0.1
eps = 1e-06


def dct_tables():
    freq = np.arange(GROUP, dtype=np.float64)[:, None]
    sample = np.arange(GROUP, dtype=np.float64)[None, :]
    factor = np.where(freq == 0, np.sqrt(1.0 / GROUP), np.sqrt(2.0 / GROUP))
    full = factor * np.cos(np.pi * (2.0 * sample + 1.0) * freq / (2.0 * GROUP))
    high = full.astype(ml_dtypes.bfloat16)
    low = (full - high.astype(np.float64)).astype(ml_dtypes.bfloat16)
    return high, low


def split(wide):
    high = wide.astype(jnp.bfloat16)
    low = (wide - high.astype(jnp.float32)).astype(jnp.bfloat16)
    return high, low


def dot(a, b, dims=(((1,), (0,)), ((), ()))):
    return lax.dot_general(a, b, dims, preferred_element_type=jnp.float32)


NT = (((1,), (1,)), ((), ()))
TN = (((0,), (0,)), ((), ()))


def gather_rows(table, blocks):
    return jnp.concatenate(
        [table[pl.ds(pl.multiple_of(lax.shift_left(b, 4), FB), FB), :] for b in blocks], axis=0
    )


def rows_of(sel, pair):
    return [lax.shift_right_logical(sel[pair * 8 + q], 3) for q in range(8)]


def cols_of(sel, pair):
    return [lax.bitwise_and(sel[pair * 8 + q], NBS - 1) for q in range(8)]


ANY = pl.BlockSpec(memory_space=pl.ANY)
VMEM = pl.BlockSpec(memory_space=pltpu.VMEM)
SMEM = pl.BlockSpec(memory_space=pltpu.SMEM)
STEP = 8
CHUNKS = HALF // STEP
CHUNK_GROUPS = 2 * STEP
UNROLL = 16


def square_kernel(g, out, buf, sem):
    chunks = sem.shape[0]
    size = g.shape[0] // chunks

    def load(c):
        part = pl.ds(c * size, size)
        return pltpu.make_async_copy(g.at[part], buf.at[part], sem.at[c])

    for c in range(chunks):
        load(c).start()

    def body(c, total):
        load(c).wait()
        wide = buf[pl.ds(c * size, size)].astype(jnp.float32)
        return total + jnp.sum((wide * wide).reshape(-1, 64, GROUP), axis=0)

    total = lax.fori_loop(0, chunks, body, jnp.zeros((64, GROUP), jnp.float32))
    out[...] = jnp.sum(total.reshape(8, 8, GROUP), axis=0)


def square_sums(grads):
    return pl.pallas_call(
        square_kernel,
        in_specs=[ANY],
        out_specs=VMEM,
        out_shape=jax.ShapeDtypeStruct((8, GROUP), jnp.float32),
        scratch_shapes=[pltpu.VMEM(grads.shape, grads.dtype), pltpu.SemaphoreType.DMA((8,))],
        compiler_params=pltpu.CompilerParams(vmem_limit_bytes=51 << 20),
        cost_estimate=pl.CostEstimate(flops=4 << 20, bytes_accessed=4 << 20, transcendentals=0),
        name="square_sums",
    )(grads)


def load_half(arrays, bufs, sem, base):
    def load(a, c):
        return pltpu.make_async_copy(
            arrays[a].at[pl.ds(2 * base + c * CHUNK_GROUPS, CHUNK_GROUPS)],
            bufs[a].at[pl.ds(c * CHUNK_GROUPS, CHUNK_GROUPS)],
            sem.at[a, c],
        )

    for c in range(CHUNKS):
        for a in range(len(arrays)):
            load(a, c).start()

    def wait(c):
        for a in range(len(arrays)):
            load(a, c).wait()

    return wait


def forward_rows(g, m, rows, t_high, t_low):
    row_high, row_low = gather_rows(t_high, rows), gather_rows(t_low, rows)
    picked = []
    for s in range(2):
        own = slice(64 * s, 64 * s + 64)
        left = jnp.concatenate([row_high[own], row_low[own]], axis=0)
        prod = dot(left, jnp.concatenate([g[s], m[s]], axis=1))
        picked.append(prod[:64] + prod[64:])
    left = jnp.concatenate(picked, axis=0)
    return split(jnp.concatenate([left[:, :GROUP], left[:, GROUP:]], axis=0))


def forward_cols(high, low, cols, t_high, t_low):
    lane = lax.broadcasted_iota(jnp.int32, (FB, GROUP), 1) // FB
    col_high, col_low = gather_rows(t_high, cols), gather_rows(t_low, cols)
    rhs = jnp.concatenate(
        [
            jnp.concatenate([col_high, col_high], axis=1),
            jnp.concatenate([col_low, jnp.zeros_like(col_low)], axis=1),
        ],
        axis=0,
    )
    prod = dot(jnp.concatenate([high, low], axis=1), rhs, NT)
    tiles = []
    for at in (0, GROUP):
        tile = None
        for q in range(8):
            part = prod[at + FB * q : at + FB * q + FB]
            part = part[:, :GROUP] + part[:, GROUP:]
            tile = part if q == 0 else jnp.where(lane == q, part, tile)
        tiles.append(tile)
    return tiles


def forward_kernel(sel, off, g, m, t_high, t_low, cg, cm, g_buf, m_buf, sem):
    base = off[0] * HALF
    wait = load_half((g, m), (g_buf, m_buf), sem, base)

    def body(c, _):
        wait(c)
        for u in range(STEP):
            p = c * STEP + u
            pair = pl.ds(2 * p, 2)
            high, low = forward_rows(g_buf[pair], m_buf[pair], rows_of(sel, base + p), t_high, t_low)
            cg[p], cm[p] = forward_cols(high, low, cols_of(sel, base + p), t_high, t_low)
        return 0

    lax.fori_loop(0, CHUNKS, body, 0)


def forward(sel, half, grads, momentum, t_high, t_low):
    shape = jax.ShapeDtypeStruct((HALF, FB, GROUP), jnp.float32)
    buf = pltpu.VMEM((2 * HALF, GROUP, GROUP), jnp.bfloat16)
    return pl.pallas_call(
        forward_kernel,
        in_specs=[SMEM, SMEM, ANY, ANY, VMEM, VMEM],
        out_specs=[VMEM, VMEM],
        out_shape=[shape, shape],
        scratch_shapes=[buf, buf, pltpu.SemaphoreType.DMA((2, CHUNKS))],
        compiler_params=pltpu.CompilerParams(vmem_limit_bytes=51 << 20),
        cost_estimate=pl.CostEstimate(flops=2 << 30, bytes_accessed=5 << 20, transcendentals=0),
        name="forward_cosine",
    )(sel, half, grads, momentum, t_high, t_low)


def clip_of(first, second):
    square_sum = jnp.sum(first + second)
    entry_count = float(4 * 2 * PAIRS * GROUP * GROUP)
    return jnp.minimum(1.0, lax.rsqrt(jnp.full((1, GROUP), square_sum) / entry_count))


def combine_kernel(first, second, g_other, m_other, g_own, m_own, c_other, c_own, clip):
    clip[...] = clip_of(first[...], second[...])
    scale = clip[...].reshape(1, 1, GROUP)
    c_other[...] = momentum_retention * m_other[...] + scale * g_other[...]
    c_own[...] = momentum_retention * m_own[...] + scale * g_own[...]


def combine(first, second, *tiles):
    shape = jax.ShapeDtypeStruct((HALF, FB, GROUP), jnp.float32)
    return pl.pallas_call(
        combine_kernel,
        in_specs=[VMEM] * 6,
        out_specs=[VMEM] * 3,
        out_shape=[shape, shape, jax.ShapeDtypeStruct((1, GROUP), jnp.float32)],
        input_output_aliases={2: 0, 4: 1},
        compiler_params=pltpu.CompilerParams(vmem_limit_bytes=8 << 20),
        cost_estimate=pl.CostEstimate(flops=1 << 20, bytes_accessed=1 << 20, transcendentals=0),
        name="combine",
    )(first, second, *tiles)


def place_blocks(coeffs, rows):
    lane = lax.broadcasted_iota(jnp.int32, (FB, GROUP), 1) // FB
    row_of = jnp.zeros((FB, GROUP), jnp.int32)
    for q in range(8):
        row_of = jnp.where(lane == q, rows[q], row_of)
    high = coeffs.astype(jnp.bfloat16).astype(jnp.float32)
    placed = []
    for part in (high, coeffs - high):
        parts = [jnp.where(row_of == b, part, 0.0) for b in range(NBS)]
        placed.append(jnp.concatenate(parts, axis=0).astype(jnp.bfloat16))
    return placed


def decode_rows(first, second, t_left):
    high = jnp.concatenate([first[0], second[0]], axis=1)
    low = jnp.concatenate([first[1], second[1]], axis=1)
    left = dot(t_left[...], jnp.concatenate([high, low, high], axis=0))
    return split(left[:, :GROUP]), split(left[:, GROUP:])


def decode_cols(high, low, cols, t_high, t_low):
    none = jnp.zeros((64, GROUP), jnp.bfloat16)

    def both(table):
        chosen = gather_rows(table, cols)
        return jnp.concatenate(
            [
                jnp.concatenate([chosen[:64], none], axis=1),
                jnp.concatenate([none, chosen[64:]], axis=1),
            ],
            axis=0,
        )

    col_high, col_low = both(t_high), both(t_low)
    result = dot(
        jnp.concatenate([high, low, high], axis=1),
        jnp.concatenate([col_high, col_high, col_low], axis=0),
    )
    return result[:, :GROUP], result[:, GROUP:]


def decode_kernel(count, sel, off, *refs):
    arrays, refs = refs[:count], refs[count:]
    scale, coeffs, t_high, t_low, t_left = refs[:5]
    out = refs[-(count + 6)]
    bufs = refs[-(count + 5) : -5]
    out_buf, high_buf, low_buf, sem, out_sem = refs[-5:]
    base = off[0] * HALF
    wait = load_half(arrays, bufs, sem, base)

    def store(c):
        return pltpu.make_async_copy(
            out_buf.at[pl.ds(c * CHUNK_GROUPS, CHUNK_GROUPS)],
            out.at[pl.ds(2 * base + c * CHUNK_GROUPS, CHUNK_GROUPS)],
            out_sem.at[c],
        )

    def first(i, _):
        for u in range(0, UNROLL, 2):
            p = i * UNROLL + u
            placed = [place_blocks(coeffs[p + k], rows_of(sel, base + p + k)) for k in range(2)]
            for k, (high, low) in enumerate(decode_rows(*placed, t_left)):
                high_buf[p + k], low_buf[p + k] = high, low
        return 0

    def second(i, _):
        chunks = UNROLL // STEP
        for k in range(chunks):
            wait(i * chunks + k)
        for u in range(UNROLL):
            p = i * UNROLL + u
            cols = cols_of(sel, base + p)
            for s, taken in enumerate(decode_cols(high_buf[p], low_buf[p], cols, t_high, t_low)):
                wide = bufs[0][2 * p + s].astype(jnp.float32)
                if count == 2:
                    wide = momentum_retention * bufs[1][2 * p + s].astype(jnp.float32) + scale[...] * wide
                out_buf[2 * p + s] = (wide - taken).astype(jnp.bfloat16)
            if (u + 1) % STEP == 0:
                store(i * chunks + u // STEP).start()
        return 0

    lax.fori_loop(0, HALF // UNROLL, first, 0)
    lax.fori_loop(0, HALF // UNROLL, second, 0)
    for c in range(CHUNKS):
        store(c).wait()


def decode_half(sel, half, arrays, scale, coeffs, tables, before, name):
    operands = (sel, half, *arrays, scale, coeffs, *tables)
    specs = [SMEM, SMEM] + [ANY] * len(arrays) + [VMEM] * 5
    aliases = {}
    if before is not None:
        aliases = {len(operands): 0}
        operands += (before,)
        specs.append(ANY)
    buf = pltpu.VMEM((2 * HALF, GROUP, GROUP), jnp.bfloat16)
    return pl.pallas_call(
        functools.partial(decode_kernel, len(arrays)),
        in_specs=specs,
        out_specs=ANY,
        out_shape=jax.ShapeDtypeStruct((2 * PAIRS, GROUP, GROUP), jnp.bfloat16),
        scratch_shapes=[buf] * (len(arrays) + 1)
        + [pltpu.VMEM((HALF, GROUP, GROUP), jnp.bfloat16)] * 2
        + [pltpu.SemaphoreType.DMA((len(arrays), CHUNKS)), pltpu.SemaphoreType.DMA((CHUNKS,))],
        input_output_aliases=aliases,
        compiler_params=pltpu.CompilerParams(vmem_limit_bytes=51 << 20),
        cost_estimate=pl.CostEstimate(flops=2 << 30, bytes_accessed=(2 << 20) * (1 + len(arrays)), transcendentals=0),
        name=name,
    )(*operands)


def total_kernel(parts, out):
    total = jnp.sum(parts[...], axis=0)
    lane = lax.broadcasted_iota(jnp.int32, (FB, GROUP), 1)
    square = total * total
    first = jnp.sum(jnp.where(lane < 64, square, 0.0))
    second = jnp.sum(jnp.where(lane < 64, 0.0, square))
    mean = jnp.where(lane < 64, first, second) / (GROUP * GROUP)
    out[...] = jnp.broadcast_to(learn_rate * total * lax.rsqrt(mean + eps), out.shape)


def scaled_totals(parts):
    return pl.pallas_call(
        total_kernel,
        in_specs=[VMEM],
        out_specs=VMEM,
        out_shape=jax.ShapeDtypeStruct((CHIPS, FB, GROUP), jnp.float32),
        compiler_params=pltpu.CompilerParams(vmem_limit_bytes=8 << 20),
        cost_estimate=pl.CostEstimate(flops=1 << 20, bytes_accessed=1 << 19, transcendentals=0),
        name="scaled_totals",
    )(parts)


def per_device(grads, momentum, weight, select):
    high, low = dct_tables()
    left = np.concatenate([high.T, high.T, low.T], axis=1)
    t_high, t_low, t_left = tables = tuple(jnp.asarray(table) for table in (high, low, left))
    grads, momentum = grads[0], momentum[0]
    sel = select.reshape(-1)
    own = lax.rem(lax.axis_index("rep"), 2).astype(jnp.int32).reshape(1)
    other = 1 - own
    same_core = [list(range(c, REPS, 2)) for c in range(2)]
    swap_core = [(i, i ^ 1) for i in range(REPS)]
    swap = lambda x: lax.ppermute(x, "rep", swap_core)
    exchange = lambda x: lax.all_to_all(x, "rep", 0, 0, tiled=True, axis_index_groups=same_core)

    sums = square_sums(grads)
    sums += lax.ppermute(sums, "mdl", [(i, i ^ 1) for i in range(4)])
    g_other, m_other = forward(sel, other, grads, momentum, t_high, t_low)
    sums, g_other, m_other = lax.optimization_barrier((sums, g_other, m_other))
    far = lax.ppermute(sums, "mdl", [(i, i ^ 2) for i in range(4)])
    g_own, m_own = forward(sel, own, grads, momentum, t_high, t_low)
    c_other, c_own, clip = combine(sums, far, g_other, m_other, g_own, m_own)
    chip, c_other, c_own = lax.optimization_barrier((c_own + swap(c_other), c_other, c_own))
    parts = exchange(chip)
    new_momentum = decode_half(
        sel, other, (grads, momentum), clip, c_other, tables, None, "momentum_other"
    )
    parts, new_momentum = lax.optimization_barrier((parts, new_momentum))
    mine, c_own = lax.optimization_barrier((scaled_totals(parts), c_own))
    totals_own = exchange(mine)
    new_momentum = decode_half(
        sel, own, (grads, momentum), clip, c_own, tables, new_momentum, "momentum_own"
    )
    totals_own, new_momentum = lax.optimization_barrier((totals_own, new_momentum))
    totals_other = swap(totals_own)
    new_weight = decode_half(sel, own, (weight,), clip, totals_own, tables, None, "weight_own")
    new_weight = decode_half(
        sel, other, (weight,), clip, totals_other, tables, new_weight, "weight_other"
    )
    return (new_weight, new_momentum[None])


def solution(mesh):
    return jax.shard_map(
        per_device,
        mesh=mesh,
        in_specs=(
            P("rep", "mdl", None, None),
            P("rep", "mdl", None, None),
            P("mdl", None, None),
            P("mdl", None),
        ),
        out_specs=(P("mdl", None, None), P("rep", "mdl", None, None)),
        check_vma=False,
    )
```

```python
import functools

import jax
import jax.numpy as jnp
import ml_dtypes
import numpy as np
from jax import lax
from jax.experimental import pallas as pl
from jax.experimental.pallas import tpu as pltpu
from jax.sharding import PartitionSpec as P

GROUP = 128
FB = 16
NBS = 8
KSEL = 4
REPS = 64
CHIPS = 32
PAIRS = 64
HALF = 32
momentum_retention = 0.9
learn_rate = 0.1
eps = 1e-06


def dct_tables():
    freq = np.arange(GROUP, dtype=np.float64)[:, None]
    sample = np.arange(GROUP, dtype=np.float64)[None, :]
    factor = np.where(freq == 0, np.sqrt(1.0 / GROUP), np.sqrt(2.0 / GROUP))
    full = factor * np.cos(np.pi * (2.0 * sample + 1.0) * freq / (2.0 * GROUP))
    high = full.astype(ml_dtypes.bfloat16)
    low = (full - high.astype(np.float64)).astype(ml_dtypes.bfloat16)
    return high, low


def split(wide):
    high = wide.astype(jnp.bfloat16)
    low = (wide - high.astype(jnp.float32)).astype(jnp.bfloat16)
    return high, low


def dot(a, b, dims=(((1,), (0,)), ((), ()))):
    return lax.dot_general(a, b, dims, preferred_element_type=jnp.float32)


NT = (((1,), (1,)), ((), ()))
TN = (((0,), (0,)), ((), ()))


def gather_rows(table, blocks):
    return jnp.concatenate(
        [table[pl.ds(pl.multiple_of(lax.shift_left(b, 4), FB), FB), :] for b in blocks], axis=0
    )


def rows_of(sel, pair):
    return [lax.shift_right_logical(sel[pair * 8 + q], 3) for q in range(8)]


def cols_of(sel, pair):
    return [lax.bitwise_and(sel[pair * 8 + q], NBS - 1) for q in range(8)]


ANY = pl.BlockSpec(memory_space=pl.ANY)
VMEM = pl.BlockSpec(memory_space=pltpu.VMEM)
SMEM = pl.BlockSpec(memory_space=pltpu.SMEM)
STEP = 8
CHUNKS = HALF // STEP
CHUNK_GROUPS = 2 * STEP
UNROLL = 16


def square_kernel(g, out, buf, sem):
    chunks = sem.shape[0]
    size = g.shape[0] // chunks

    def load(c):
        part = pl.ds(c * size, size)
        return pltpu.make_async_copy(g.at[part], buf.at[part], sem.at[c])

    for c in range(chunks):
        load(c).start()

    def body(c, total):
        load(c).wait()
        wide = buf[pl.ds(c * size, size)].astype(jnp.float32)
        return total + jnp.sum((wide * wide).reshape(-1, 64, GROUP), axis=0)

    total = lax.fori_loop(0, chunks, body, jnp.zeros((64, GROUP), jnp.float32))
    out[...] = jnp.sum(total.reshape(8, 8, GROUP), axis=0)


def square_sums(grads):
    return pl.pallas_call(
        square_kernel,
        in_specs=[ANY],
        out_specs=VMEM,
        out_shape=jax.ShapeDtypeStruct((8, GROUP), jnp.float32),
        scratch_shapes=[pltpu.VMEM(grads.shape, grads.dtype), pltpu.SemaphoreType.DMA((8,))],
        compiler_params=pltpu.CompilerParams(vmem_limit_bytes=51 << 20),
        cost_estimate=pl.CostEstimate(flops=4 << 20, bytes_accessed=4 << 20, transcendentals=0),
        name="square_sums",
    )(grads)


def load_half(arrays, bufs, sem, base):
    def load(a, c):
        return pltpu.make_async_copy(
            arrays[a].at[pl.ds(2 * base + c * CHUNK_GROUPS, CHUNK_GROUPS)],
            bufs[a].at[pl.ds(c * CHUNK_GROUPS, CHUNK_GROUPS)],
            sem.at[a, c],
        )

    for c in range(CHUNKS):
        for a in range(len(arrays)):
            load(a, c).start()

    def wait(c):
        for a in range(len(arrays)):
            load(a, c).wait()

    return wait


def forward_rows(g, m, rows, t_high, t_low):
    row_high, row_low = gather_rows(t_high, rows), gather_rows(t_low, rows)
    picked = []
    for s in range(2):
        own = slice(64 * s, 64 * s + 64)
        left = jnp.concatenate([row_high[own], row_low[own]], axis=0)
        prod = dot(left, jnp.concatenate([g[s], m[s]], axis=1))
        picked.append(prod[:64] + prod[64:])
    left = jnp.concatenate(picked, axis=0)
    return split(jnp.concatenate([left[:, :GROUP], left[:, GROUP:]], axis=0))


def forward_cols(high, low, cols, t_high, t_low):
    lane = lax.broadcasted_iota(jnp.int32, (FB, GROUP), 1) // FB
    col_high, col_low = gather_rows(t_high, cols), gather_rows(t_low, cols)
    rhs = jnp.concatenate(
        [
            jnp.concatenate([col_high, col_high], axis=1),
            jnp.concatenate([col_low, jnp.zeros_like(col_low)], axis=1),
        ],
        axis=0,
    )
    prod = dot(jnp.concatenate([high, low], axis=1), rhs, NT)
    tiles = []
    for at in (0, GROUP):
        tile = None
        for q in range(8):
            part = prod[at + FB * q : at + FB * q + FB]
            part = part[:, :GROUP] + part[:, GROUP:]
            tile = part if q == 0 else jnp.where(lane == q, part, tile)
        tiles.append(tile)
    return tiles


def forward_kernel(sel, off, g, m, t_high, t_low, cg, cm, g_buf, m_buf, sem):
    base = off[0] * HALF
    wait = load_half((g, m), (g_buf, m_buf), sem, base)

    def body(c, _):
        wait(c)
        for u in range(STEP):
            p = c * STEP + u
            pair = pl.ds(2 * p, 2)
            high, low = forward_rows(g_buf[pair], m_buf[pair], rows_of(sel, base + p), t_high, t_low)
            cg[p], cm[p] = forward_cols(high, low, cols_of(sel, base + p), t_high, t_low)
        return 0

    lax.fori_loop(0, CHUNKS, body, 0)


def forward(sel, half, grads, momentum, t_high, t_low):
    shape = jax.ShapeDtypeStruct((HALF, FB, GROUP), jnp.float32)
    buf = pltpu.VMEM((2 * HALF, GROUP, GROUP), jnp.bfloat16)
    return pl.pallas_call(
        forward_kernel,
        in_specs=[SMEM, SMEM, ANY, ANY, VMEM, VMEM],
        out_specs=[VMEM, VMEM],
        out_shape=[shape, shape],
        scratch_shapes=[buf, buf, pltpu.SemaphoreType.DMA((2, CHUNKS))],
        compiler_params=pltpu.CompilerParams(vmem_limit_bytes=51 << 20),
        cost_estimate=pl.CostEstimate(flops=2 << 30, bytes_accessed=5 << 20, transcendentals=0),
        name="forward_cosine",
    )(sel, half, grads, momentum, t_high, t_low)


def clip_of(first, second):
    square_sum = jnp.sum(first + second)
    entry_count = float(4 * 2 * PAIRS * GROUP * GROUP)
    return jnp.minimum(1.0, lax.rsqrt(jnp.full((1, GROUP), square_sum) / entry_count))


def combine_kernel(first, second, g_other, m_other, g_own, m_own, c_other, c_own, clip):
    clip[...] = clip_of(first[...], second[...])
    scale = clip[...].reshape(1, 1, GROUP)
    c_other[...] = momentum_retention * m_other[...] + scale * g_other[...]
    c_own[...] = momentum_retention * m_own[...] + scale * g_own[...]


def combine(first, second, *tiles):
    shape = jax.ShapeDtypeStruct((HALF, FB, GROUP), jnp.float32)
    return pl.pallas_call(
        combine_kernel,
        in_specs=[VMEM] * 6,
        out_specs=[VMEM] * 3,
        out_shape=[shape, shape, jax.ShapeDtypeStruct((1, GROUP), jnp.float32)],
        input_output_aliases={2: 0, 4: 1},
        compiler_params=pltpu.CompilerParams(vmem_limit_bytes=8 << 20),
        cost_estimate=pl.CostEstimate(flops=1 << 20, bytes_accessed=1 << 20, transcendentals=0),
        name="combine",
    )(first, second, *tiles)


def place_blocks(coeffs, rows):
    lane = lax.broadcasted_iota(jnp.int32, (FB, GROUP), 1) // FB
    row_of = jnp.zeros((FB, GROUP), jnp.int32)
    for q in range(8):
        row_of = jnp.where(lane == q, rows[q], row_of)
    high = coeffs.astype(jnp.bfloat16).astype(jnp.float32)
    placed = []
    for part in (high, coeffs - high):
        parts = [jnp.where(row_of == b, part, 0.0) for b in range(NBS)]
        placed.append(jnp.concatenate(parts, axis=0).astype(jnp.bfloat16))
    return placed


def decode_rows(first, second, t_left):
    high = jnp.concatenate([first[0], second[0]], axis=1)
    low = jnp.concatenate([first[1], second[1]], axis=1)
    left = dot(t_left[...], jnp.concatenate([high, low, high], axis=0))
    return split(left[:, :GROUP]), split(left[:, GROUP:])


def decode_cols(high, low, cols, t_high, t_low):
    none = jnp.zeros((64, GROUP), jnp.bfloat16)

    def both(table):
        chosen = gather_rows(table, cols)
        return jnp.concatenate(
            [
                jnp.concatenate([chosen[:64], none], axis=1),
                jnp.concatenate([none, chosen[64:]], axis=1),
            ],
            axis=0,
        )

    col_high, col_low = both(t_high), both(t_low)
    result = dot(
        jnp.concatenate([high, low, high], axis=1),
        jnp.concatenate([col_high, col_high, col_low], axis=0),
    )
    return result[:, :GROUP], result[:, GROUP:]


def decode_kernel(count, sel, off, *refs):
    arrays, refs = refs[:count], refs[count:]
    scale, coeffs, t_high, t_low, t_left = refs[:5]
    out = refs[-(count + 6)]
    bufs = refs[-(count + 5) : -5]
    out_buf, high_buf, low_buf, sem, out_sem = refs[-5:]
    base = off[0] * HALF
    wait = load_half(arrays, bufs, sem, base)

    def store(c):
        return pltpu.make_async_copy(
            out_buf.at[pl.ds(c * CHUNK_GROUPS, CHUNK_GROUPS)],
            out.at[pl.ds(2 * base + c * CHUNK_GROUPS, CHUNK_GROUPS)],
            out_sem.at[c],
        )

    def first(i, _):
        for u in range(0, UNROLL, 2):
            p = i * UNROLL + u
            placed = [place_blocks(coeffs[p + k], rows_of(sel, base + p + k)) for k in range(2)]
            for k, (high, low) in enumerate(decode_rows(*placed, t_left)):
                high_buf[p + k], low_buf[p + k] = high, low
        return 0

    def second(i, _):
        chunks = UNROLL // STEP
        for k in range(chunks):
            wait(i * chunks + k)
        for u in range(UNROLL):
            p = i * UNROLL + u
            cols = cols_of(sel, base + p)
            for s, taken in enumerate(decode_cols(high_buf[p], low_buf[p], cols, t_high, t_low)):
                wide = bufs[0][2 * p + s].astype(jnp.float32)
                if count == 2:
                    wide = momentum_retention * bufs[1][2 * p + s].astype(jnp.float32) + scale[...] * wide
                out_buf[2 * p + s] = (wide - taken).astype(jnp.bfloat16)
            if (u + 1) % STEP == 0:
                store(i * chunks + u // STEP).start()
        return 0

    lax.fori_loop(0, HALF // UNROLL, first, 0)
    lax.fori_loop(0, HALF // UNROLL, second, 0)
    for c in range(CHUNKS):
        store(c).wait()


def decode_half(sel, half, arrays, scale, coeffs, tables, before, name):
    operands = (sel, half, *arrays, scale, coeffs, *tables)
    specs = [SMEM, SMEM] + [ANY] * len(arrays) + [VMEM] * 5
    aliases = {}
    if before is not None:
        aliases = {len(operands): 0}
        operands += (before,)
        specs.append(ANY)
    buf = pltpu.VMEM((2 * HALF, GROUP, GROUP), jnp.bfloat16)
    return pl.pallas_call(
        functools.partial(decode_kernel, len(arrays)),
        in_specs=specs,
        out_specs=ANY,
        out_shape=jax.ShapeDtypeStruct((2 * PAIRS, GROUP, GROUP), jnp.bfloat16),
        scratch_shapes=[buf] * (len(arrays) + 1)
        + [pltpu.VMEM((HALF, GROUP, GROUP), jnp.bfloat16)] * 2
        + [pltpu.SemaphoreType.DMA((len(arrays), CHUNKS)), pltpu.SemaphoreType.DMA((CHUNKS,))],
        input_output_aliases=aliases,
        compiler_params=pltpu.CompilerParams(vmem_limit_bytes=51 << 20),
        cost_estimate=pl.CostEstimate(flops=2 << 30, bytes_accessed=(2 << 20) * (1 + len(arrays)), transcendentals=0),
        name=name,
    )(*operands)


def total_kernel(parts, out):
    total = jnp.sum(parts[...], axis=0)
    lane = lax.broadcasted_iota(jnp.int32, (FB, GROUP), 1)
    square = total * total
    first = jnp.sum(jnp.where(lane < 64, square, 0.0))
    second = jnp.sum(jnp.where(lane < 64, 0.0, square))
    mean = jnp.where(lane < 64, first, second) / (GROUP * GROUP)
    out[...] = jnp.broadcast_to(learn_rate * total * lax.rsqrt(mean + eps), out.shape)


def scaled_totals(parts):
    return pl.pallas_call(
        total_kernel,
        in_specs=[VMEM],
        out_specs=VMEM,
        out_shape=jax.ShapeDtypeStruct((CHIPS, FB, GROUP), jnp.float32),
        compiler_params=pltpu.CompilerParams(vmem_limit_bytes=8 << 20),
        cost_estimate=pl.CostEstimate(flops=1 << 20, bytes_accessed=1 << 19, transcendentals=0),
        name="scaled_totals",
    )(parts)


def per_device(grads, momentum, weight, select):
    high, low = dct_tables()
    left = np.concatenate([high.T, high.T, low.T], axis=1)
    t_high, t_low, t_left = tables = tuple(jnp.asarray(table) for table in (high, low, left))
    grads, momentum = grads[0], momentum[0]
    sel = select.reshape(-1)
    own = lax.rem(lax.axis_index("rep"), 2).astype(jnp.int32).reshape(1)
    other = 1 - own
    same_core = [[(c + 2 * (18 + k)) % REPS for k in range(CHIPS)] for c in range(2)]
    swap_core = [(i, i ^ 1) for i in range(REPS)]
    swap = lambda x: lax.ppermute(x, "rep", swap_core)
    exchange = lambda x: lax.all_to_all(x, "rep", 0, 0, tiled=True, axis_index_groups=same_core)

    sums = square_sums(grads)
    sums += lax.ppermute(sums, "mdl", [(i, i ^ 1) for i in range(4)])
    g_other, m_other = forward(sel, other, grads, momentum, t_high, t_low)
    sums, g_other, m_other = lax.optimization_barrier((sums, g_other, m_other))
    far = lax.ppermute(sums, "mdl", [(i, i ^ 2) for i in range(4)])
    g_own, m_own = forward(sel, own, grads, momentum, t_high, t_low)
    c_other, c_own, clip = combine(sums, far, g_other, m_other, g_own, m_own)
    chip, c_other, c_own = lax.optimization_barrier((c_own + swap(c_other), c_other, c_own))
    parts = exchange(chip)
    new_momentum = decode_half(
        sel, other, (grads, momentum), clip, c_other, tables, None, "momentum_other"
    )
    parts, new_momentum = lax.optimization_barrier((parts, new_momentum))
    mine, c_own = lax.optimization_barrier((scaled_totals(parts), c_own))
    totals_own = exchange(mine)
    new_momentum = decode_half(
        sel, own, (grads, momentum), clip, c_own, tables, new_momentum, "momentum_own"
    )
    totals_own, new_momentum = lax.optimization_barrier((totals_own, new_momentum))
    totals_other = swap(totals_own)
    new_weight = decode_half(sel, own, (weight,), clip, totals_own, tables, None, "weight_own")
    new_weight = decode_half(
        sel, other, (weight,), clip, totals_other, tables, new_weight, "weight_other"
    )
    return (new_weight, new_momentum[None])


def solution(mesh):
    return jax.shard_map(
        per_device,
        mesh=mesh,
        in_specs=(
            P("rep", "mdl", None, None),
            P("rep", "mdl", None, None),
            P("mdl", None, None),
            P("mdl", None),
        ),
        out_specs=(P("mdl", None, None), P("rep", "mdl", None, None)),
        check_vma=False,
    )
```

```python
import functools

import jax
import jax.numpy as jnp
import ml_dtypes
import numpy as np
from jax import lax
from jax.experimental import pallas as pl
from jax.experimental.pallas import tpu as pltpu
from jax.sharding import PartitionSpec as P

GROUP = 128
FB = 16
NBS = 8
KSEL = 4
REPS = 64
CHIPS = 32
PAIRS = 64
HALF = 32
momentum_retention = 0.9
learn_rate = 0.1
eps = 1e-06


def dct_tables():
    freq = np.arange(GROUP, dtype=np.float64)[:, None]
    sample = np.arange(GROUP, dtype=np.float64)[None, :]
    factor = np.where(freq == 0, np.sqrt(1.0 / GROUP), np.sqrt(2.0 / GROUP))
    full = factor * np.cos(np.pi * (2.0 * sample + 1.0) * freq / (2.0 * GROUP))
    high = full.astype(ml_dtypes.bfloat16)
    low = (full - high.astype(np.float64)).astype(ml_dtypes.bfloat16)
    return high, low


def split(wide):
    high = wide.astype(jnp.bfloat16)
    low = (wide - high.astype(jnp.float32)).astype(jnp.bfloat16)
    return high, low


def dot(a, b, dims=(((1,), (0,)), ((), ()))):
    return lax.dot_general(a, b, dims, preferred_element_type=jnp.float32)


NT = (((1,), (1,)), ((), ()))
TN = (((0,), (0,)), ((), ()))


def gather_rows(table, blocks):
    return jnp.concatenate(
        [table[pl.ds(pl.multiple_of(lax.shift_left(b, 4), FB), FB), :] for b in blocks], axis=0
    )


def rows_of(sel, pair):
    return [lax.shift_right_logical(sel[pair * 8 + q], 3) for q in range(8)]


def cols_of(sel, pair):
    return [lax.bitwise_and(sel[pair * 8 + q], NBS - 1) for q in range(8)]


ANY = pl.BlockSpec(memory_space=pl.ANY)
VMEM = pl.BlockSpec(memory_space=pltpu.VMEM)
SMEM = pl.BlockSpec(memory_space=pltpu.SMEM)
STEP = 8
CHUNKS = HALF // STEP
CHUNK_GROUPS = 2 * STEP
UNROLL = 16


def square_kernel(g, out, buf, sem):
    chunks = sem.shape[0]
    size = g.shape[0] // chunks

    def load(c):
        part = pl.ds(c * size, size)
        return pltpu.make_async_copy(g.at[part], buf.at[part], sem.at[c])

    for c in range(chunks):
        load(c).start()

    def body(c, total):
        load(c).wait()
        wide = buf[pl.ds(c * size, size)].astype(jnp.float32)
        return total + jnp.sum((wide * wide).reshape(-1, 64, GROUP), axis=0)

    total = lax.fori_loop(0, chunks, body, jnp.zeros((64, GROUP), jnp.float32))
    out[...] = jnp.sum(total.reshape(8, 8, GROUP), axis=0)


def square_sums(grads):
    return pl.pallas_call(
        square_kernel,
        in_specs=[ANY],
        out_specs=VMEM,
        out_shape=jax.ShapeDtypeStruct((8, GROUP), jnp.float32),
        scratch_shapes=[pltpu.VMEM(grads.shape, grads.dtype), pltpu.SemaphoreType.DMA((8,))],
        compiler_params=pltpu.CompilerParams(vmem_limit_bytes=51 << 20),
        cost_estimate=pl.CostEstimate(flops=4 << 20, bytes_accessed=4 << 20, transcendentals=0),
        name="square_sums",
    )(grads)


def half_base(swapped):
    core = lax.rem(lax.axis_index("rep"), 2)
    return (1 - core if swapped else core) * HALF


def load_half(arrays, bufs, sem, base):
    def load(a, c):
        return pltpu.make_async_copy(
            arrays[a].at[pl.ds(2 * base + c * CHUNK_GROUPS, CHUNK_GROUPS)],
            bufs[a].at[pl.ds(c * CHUNK_GROUPS, CHUNK_GROUPS)],
            sem.at[a, c],
        )

    for c in range(CHUNKS):
        for a in range(len(arrays)):
            load(a, c).start()

    def wait(c):
        for a in range(len(arrays)):
            load(a, c).wait()

    return wait


def forward_rows(g, m, rows, t_high, t_low):
    row_high, row_low = gather_rows(t_high, rows), gather_rows(t_low, rows)
    picked = []
    for s in range(2):
        own = slice(64 * s, 64 * s + 64)
        left = jnp.concatenate([row_high[own], row_low[own]], axis=0)
        prod = dot(left, jnp.concatenate([g[s], m[s]], axis=1))
        picked.append(prod[:64] + prod[64:])
    left = jnp.concatenate(picked, axis=0)
    return split(jnp.concatenate([left[:, :GROUP], left[:, GROUP:]], axis=0))


def forward_cols(highs, lows, cols, t_right):
    lane = lax.broadcasted_iota(jnp.int32, (FB, GROUP), 1) // FB
    lhs = jnp.concatenate([jnp.concatenate(highs, axis=0), jnp.concatenate(lows, axis=0)], axis=1)
    prod = dot(lhs, t_right[...])
    prod = prod[:, :GROUP] + prod[:, GROUP:]
    result = []
    for k, col in enumerate(cols):
        tiles = []
        for at in (2 * k * GROUP, (2 * k + 1) * GROUP):
            tile = None
            for q in range(8):
                shift = lax.bitwise_and(FB * q - lax.shift_left(col[q], 4), GROUP - 1)
                part = pltpu.roll(prod[at + FB * q : at + FB * q + FB], shift, 1)
                tile = part if q == 0 else jnp.where(lane == q, part, tile)
            tiles.append(tile)
        result.append(tiles)
    return result


def forward_kernel(swapped, sel_in, g, m, t_high, t_low, t_right, cg, cm, g_buf, m_buf, sel, sem, sel_sem):
    base = half_base(swapped)
    picked = pltpu.make_async_copy(sel_in, sel, sel_sem)
    picked.start()
    wait = load_half((g, m), (g_buf, m_buf), sem, base)
    picked.wait()

    def body(i, _):
        highs, lows = [], []
        for u in range(UNROLL):
            p = i * UNROLL + u
            if u % STEP == 0:
                wait(i * (UNROLL // STEP) + u // STEP)
            pair = pl.ds(2 * p, 2)
            high, low = forward_rows(g_buf[pair], m_buf[pair], rows_of(sel, base + p), t_high, t_low)
            highs.append(high)
            lows.append(low)
        for u in range(0, UNROLL, 2):
            p = i * UNROLL + u
            cols = [cols_of(sel, base + p + k) for k in range(2)]
            tiles = forward_cols(highs[u : u + 2], lows[u : u + 2], cols, t_right)
            for k in range(2):
                cg[p + k], cm[p + k] = tiles[k]
        return 0

    lax.fori_loop(0, HALF // UNROLL, body, 0)


def forward(sel, swapped, grads, momentum, *tables):
    shape = jax.ShapeDtypeStruct((HALF, FB, GROUP), jnp.float32)
    buf = pltpu.VMEM((2 * HALF, GROUP, GROUP), jnp.bfloat16)
    return pl.pallas_call(
        functools.partial(forward_kernel, swapped),
        in_specs=[ANY] * 3 + [VMEM] * 3,
        out_specs=[VMEM, VMEM],
        out_shape=[shape, shape],
        scratch_shapes=[
            buf,
            buf,
            pltpu.SMEM((2 * PAIRS * KSEL,), jnp.int32),
            pltpu.SemaphoreType.DMA((2, CHUNKS)),
            pltpu.SemaphoreType.DMA,
        ],
        compiler_params=pltpu.CompilerParams(vmem_limit_bytes=51 << 20),
        cost_estimate=pl.CostEstimate(flops=2 << 30, bytes_accessed=5 << 20, transcendentals=0),
        name="forward_cosine",
    )(sel, grads, momentum, *tables)


def clip_of(first, second):
    square_sum = jnp.sum(first + second)
    entry_count = float(4 * 2 * PAIRS * GROUP * GROUP)
    return jnp.minimum(1.0, lax.rsqrt(jnp.full((1, GROUP), square_sum) / entry_count))


def combine_kernel(first, second, g_other, m_other, g_own, m_own, c_other, c_own, clip):
    clip[...] = clip_of(first[...], second[...])
    scale = clip[...].reshape(1, 1, GROUP)
    c_other[...] = momentum_retention * m_other[...] + scale * g_other[...]
    c_own[...] = momentum_retention * m_own[...] + scale * g_own[...]


def combine(first, second, *tiles):
    shape = jax.ShapeDtypeStruct((HALF, FB, GROUP), jnp.float32)
    return pl.pallas_call(
        combine_kernel,
        in_specs=[VMEM] * 6,
        out_specs=[VMEM] * 3,
        out_shape=[shape, shape, jax.ShapeDtypeStruct((1, GROUP), jnp.float32)],
        input_output_aliases={2: 0, 4: 1},
        compiler_params=pltpu.CompilerParams(vmem_limit_bytes=8 << 20),
        cost_estimate=pl.CostEstimate(flops=1 << 20, bytes_accessed=1 << 20, transcendentals=0),
        name="combine",
    )(first, second, *tiles)


def place_blocks(coeffs, row_of):
    row_of = jnp.broadcast_to(row_of, coeffs.shape)
    high = coeffs.astype(jnp.bfloat16).astype(jnp.float32)
    placed = []
    for part in (high, coeffs - high):
        parts = [jnp.where(row_of == b, part, 0.0) for b in range(NBS)]
        placed.append(jnp.concatenate(parts, axis=0).astype(jnp.bfloat16))
    return placed


def decode_rows(first, second, t_left):
    high = jnp.concatenate([first[0], second[0]], axis=1)
    low = jnp.concatenate([first[1], second[1]], axis=1)
    left = dot(t_left[...], jnp.concatenate([high, low, high], axis=0))
    return split(left[:, :GROUP]), split(left[:, GROUP:])


def decode_cols(high, low, cols, t_high, t_low):
    none = jnp.zeros((64, GROUP), jnp.bfloat16)

    def both(table):
        chosen = gather_rows(table, cols)
        return jnp.concatenate(
            [
                jnp.concatenate([chosen[:64], none], axis=1),
                jnp.concatenate([none, chosen[64:]], axis=1),
            ],
            axis=0,
        )

    col_high, col_low = both(t_high), both(t_low)
    result = dot(
        jnp.concatenate([high, low, high], axis=1),
        jnp.concatenate([col_high, col_high, col_low], axis=0),
    )
    return result[:, :GROUP], result[:, GROUP:]


def decode_kernel(count, swapped, sel_in, *refs):
    arrays, refs = refs[:count], refs[count:]
    scale, coeffs, row_of, t_high, t_low, t_left = refs[:6]
    out = refs[-(count + 8)]
    bufs = refs[-(count + 7) : -7]
    out_buf, high_buf, low_buf, sel, sem, out_sem, sel_sem = refs[-7:]
    base = half_base(swapped)
    picked = pltpu.make_async_copy(sel_in, sel, sel_sem)
    picked.start()
    wait = load_half(arrays, bufs, sem, base)

    def store(c):
        return pltpu.make_async_copy(
            out_buf.at[pl.ds(c * CHUNK_GROUPS, CHUNK_GROUPS)],
            out.at[pl.ds(2 * base + c * CHUNK_GROUPS, CHUNK_GROUPS)],
            out_sem.at[c],
        )

    def first(i, _):
        for u in range(0, UNROLL, 2):
            p = i * UNROLL + u
            placed = [place_blocks(coeffs[p + k], row_of[pl.ds(base + p + k, 1)]) for k in range(2)]
            for k, (high, low) in enumerate(decode_rows(*placed, t_left)):
                high_buf[p + k], low_buf[p + k] = high, low
        return 0

    def second(i, _):
        chunks = UNROLL // STEP
        for k in range(chunks):
            wait(i * chunks + k)
        for u in range(UNROLL):
            p = i * UNROLL + u
            cols = cols_of(sel, base + p)
            for s, taken in enumerate(decode_cols(high_buf[p], low_buf[p], cols, t_high, t_low)):
                wide = bufs[0][2 * p + s].astype(jnp.float32)
                if count == 2:
                    wide = momentum_retention * bufs[1][2 * p + s].astype(jnp.float32) + scale[...] * wide
                out_buf[2 * p + s] = (wide - taken).astype(jnp.bfloat16)
            if (u + 1) % STEP == 0:
                store(i * chunks + u // STEP).start()
        return 0

    lax.fori_loop(0, HALF // UNROLL, first, 0)
    picked.wait()
    lax.fori_loop(0, HALF // UNROLL, second, 0)
    for c in range(CHUNKS):
        store(c).wait()


def decode_half(sel, swapped, arrays, scale, coeffs, row_of, tables, before, name):
    operands = (sel, *arrays, scale, coeffs, row_of, *tables)
    specs = [ANY] + [ANY] * len(arrays) + [VMEM] * 6
    aliases = {}
    if before is not None:
        aliases = {len(operands): 0}
        operands += (before,)
        specs.append(ANY)
    buf = pltpu.VMEM((2 * HALF, GROUP, GROUP), jnp.bfloat16)
    return pl.pallas_call(
        functools.partial(decode_kernel, len(arrays), swapped),
        in_specs=specs,
        out_specs=ANY,
        out_shape=jax.ShapeDtypeStruct((2 * PAIRS, GROUP, GROUP), jnp.bfloat16),
        scratch_shapes=[buf] * (len(arrays) + 1)
        + [pltpu.VMEM((HALF, GROUP, GROUP), jnp.bfloat16)] * 2
        + [
            pltpu.SMEM((2 * PAIRS * KSEL,), jnp.int32),
            pltpu.SemaphoreType.DMA((len(arrays), CHUNKS)),
            pltpu.SemaphoreType.DMA((CHUNKS,)),
            pltpu.SemaphoreType.DMA,
        ],
        input_output_aliases=aliases,
        compiler_params=pltpu.CompilerParams(vmem_limit_bytes=51 << 20),
        cost_estimate=pl.CostEstimate(flops=2 << 30, bytes_accessed=(2 << 20) * (1 + len(arrays)), transcendentals=0),
        name=name,
    )(*operands)


def total_kernel(parts, out):
    total = jnp.sum(parts[...], axis=0)
    lane = lax.broadcasted_iota(jnp.int32, (FB, GROUP), 1)
    square = total * total
    first = jnp.sum(jnp.where(lane < 64, square, 0.0))
    second = jnp.sum(jnp.where(lane < 64, 0.0, square))
    mean = jnp.where(lane < 64, first, second) / (GROUP * GROUP)
    out[...] = jnp.broadcast_to(learn_rate * total * lax.rsqrt(mean + eps), out.shape)


def scaled_totals(parts):
    return pl.pallas_call(
        total_kernel,
        in_specs=[VMEM],
        out_specs=VMEM,
        out_shape=jax.ShapeDtypeStruct((CHIPS, FB, GROUP), jnp.float32),
        compiler_params=pltpu.CompilerParams(vmem_limit_bytes=8 << 20),
        cost_estimate=pl.CostEstimate(flops=1 << 20, bytes_accessed=1 << 19, transcendentals=0),
        name="scaled_totals",
    )(parts)


def per_device(grads, momentum, weight, select):
    high, low = dct_tables()
    left = np.concatenate([high.T, high.T, low.T], axis=1)
    right = np.concatenate([high.T, low.T, high.T, np.zeros_like(low)], axis=1)
    t_right = jnp.asarray(np.concatenate([right[:, : 2 * GROUP], right[:, 2 * GROUP :]], axis=0))
    t_high, t_low, t_left = tables = tuple(jnp.asarray(table) for table in (high, low, left))
    grads, momentum = grads[0], momentum[0]
    sel = select.reshape(-1)
    same_core = [[(c + 2 * (18 + k)) % REPS for k in range(CHIPS)] for c in range(2)]
    swap_core = [(i, i ^ 1) for i in range(REPS)]
    swap = lambda x: lax.ppermute(x, "rep", swap_core)
    exchange = lambda x: lax.all_to_all(x, "rep", 0, 0, tiled=True, axis_index_groups=same_core)

    sums = square_sums(grads)
    sums += lax.ppermute(sums, "mdl", [(i, i ^ 1) for i in range(4)])
    g_other, m_other = forward(sel, True, grads, momentum, t_high, t_low, t_right)
    sums, g_other, m_other = lax.optimization_barrier((sums, g_other, m_other))
    far = lax.ppermute(sums, "mdl", [(i, i ^ 2) for i in range(4)])
    g_own, m_own = forward(sel, False, grads, momentum, t_high, t_low, t_right)
    c_other, c_own, clip = combine(sums, far, g_other, m_other, g_own, m_own)
    chip, c_other, c_own = lax.optimization_barrier((c_own + swap(c_other), c_other, c_own))
    select, _ = lax.optimization_barrier((select, chip))
    row_of = jnp.repeat(lax.shift_right_logical(select, 3), FB, axis=1).reshape(PAIRS, GROUP)
    parts = exchange(chip)
    new_momentum = decode_half(
        sel, True, (grads, momentum), clip, c_other, row_of, tables, None, "momentum_other"
    )
    parts, new_momentum = lax.optimization_barrier((parts, new_momentum))
    mine, c_own = lax.optimization_barrier((scaled_totals(parts), c_own))
    totals_own = exchange(mine)
    new_momentum = decode_half(
        sel, False, (grads, momentum), clip, c_own, row_of, tables, new_momentum, "momentum_own"
    )
    totals_own, new_momentum = lax.optimization_barrier((totals_own, new_momentum))
    totals_other = swap(totals_own)
    new_weight = decode_half(sel, False, (weight,), clip, totals_own, row_of, tables, None, "weight_own")
    new_weight = decode_half(
        sel, True, (weight,), clip, totals_other, row_of, tables, new_weight, "weight_other"
    )
    return (new_weight, new_momentum[None])


def solution(mesh):
    return jax.shard_map(
        per_device,
        mesh=mesh,
        in_specs=(
            P("rep", "mdl", None, None),
            P("rep", "mdl", None, None),
            P("mdl", None, None),
            P("mdl", None),
        ),
        out_specs=(P("mdl", None, None), P("rep", "mdl", None, None)),
        check_vma=False,
    )
```

```python
import functools

import jax
import jax.numpy as jnp
import ml_dtypes
import numpy as np
from jax import lax
from jax.experimental import pallas as pl
from jax.experimental.pallas import tpu as pltpu
from jax.sharding import PartitionSpec as P

GROUP = 128
FB = 16
NBS = 8
KSEL = 4
REPS = 64
CHIPS = 32
PAIRS = 64
HALF = 32
momentum_retention = 0.9
learn_rate = 0.1
eps = 1e-06


def dct_tables():
    freq = np.arange(GROUP, dtype=np.float64)[:, None]
    sample = np.arange(GROUP, dtype=np.float64)[None, :]
    factor = np.where(freq == 0, np.sqrt(1.0 / GROUP), np.sqrt(2.0 / GROUP))
    full = factor * np.cos(np.pi * (2.0 * sample + 1.0) * freq / (2.0 * GROUP))
    high = full.astype(ml_dtypes.bfloat16)
    low = (full - high.astype(np.float64)).astype(ml_dtypes.bfloat16)
    return high, low


def split(wide):
    high = wide.astype(jnp.bfloat16)
    low = (wide - high.astype(jnp.float32)).astype(jnp.bfloat16)
    return high, low


def dot(a, b, dims=(((1,), (0,)), ((), ()))):
    return lax.dot_general(a, b, dims, preferred_element_type=jnp.float32)


NT = (((1,), (1,)), ((), ()))
TN = (((0,), (0,)), ((), ()))


def gather_rows(table, blocks):
    return jnp.concatenate(
        [table[pl.ds(pl.multiple_of(lax.shift_left(b, 4), FB), FB), :] for b in blocks], axis=0
    )


def block_at(sel, pair, q):
    if len(sel.shape) == 1:
        return sel[pair * 8 + q]
    return sel[q % KSEL, 2 * pair + q // KSEL]


def rows_of(sel, pair):
    return [lax.shift_right_logical(block_at(sel, pair, q), 3) for q in range(8)]


def cols_of(sel, pair):
    return [lax.bitwise_and(block_at(sel, pair, q), NBS - 1) for q in range(8)]


ANY = pl.BlockSpec(memory_space=pl.ANY)
VMEM = pl.BlockSpec(memory_space=pltpu.VMEM)
SMEM = pl.BlockSpec(memory_space=pltpu.SMEM)
STEP = 8
CHUNKS = HALF // STEP
CHUNK_GROUPS = 2 * STEP
UNROLL = 16


def square_kernel(g, out, buf, sem):
    chunks = sem.shape[0]
    size = g.shape[0] // chunks

    def load(c):
        part = pl.ds(c * size, size)
        return pltpu.make_async_copy(g.at[part], buf.at[part], sem.at[c])

    for c in range(chunks):
        load(c).start()

    def body(c, total):
        load(c).wait()
        wide = buf[pl.ds(c * size, size)].astype(jnp.float32)
        return total + jnp.sum((wide * wide).reshape(-1, 64, GROUP), axis=0)

    total = lax.fori_loop(0, chunks, body, jnp.zeros((64, GROUP), jnp.float32))
    out[...] = jnp.sum(total.reshape(8, 8, GROUP), axis=0)


def square_sums(grads):
    return pl.pallas_call(
        square_kernel,
        in_specs=[ANY],
        out_specs=VMEM,
        out_shape=jax.ShapeDtypeStruct((8, GROUP), jnp.float32),
        scratch_shapes=[pltpu.VMEM(grads.shape, grads.dtype), pltpu.SemaphoreType.DMA((8,))],
        compiler_params=pltpu.CompilerParams(vmem_limit_bytes=51 << 20),
        cost_estimate=pl.CostEstimate(flops=4 << 20, bytes_accessed=4 << 20, transcendentals=0),
        name="square_sums",
    )(grads)


def half_base(swapped):
    core = lax.rem(lax.axis_index("rep"), 2)
    return (1 - core if swapped else core) * HALF


def load_half(arrays, bufs, sem, base):
    def load(a, c):
        return pltpu.make_async_copy(
            arrays[a].at[pl.ds(2 * base + c * CHUNK_GROUPS, CHUNK_GROUPS)],
            bufs[a].at[pl.ds(c * CHUNK_GROUPS, CHUNK_GROUPS)],
            sem.at[a, c],
        )

    for c in range(CHUNKS):
        for a in range(len(arrays)):
            load(a, c).start()

    def wait(c):
        for a in range(len(arrays)):
            load(a, c).wait()

    return wait


def forward_rows(g, m, rows, t_high, t_low):
    row_high, row_low = gather_rows(t_high, rows), gather_rows(t_low, rows)
    picked = []
    for s in range(2):
        own = slice(64 * s, 64 * s + 64)
        left = jnp.concatenate([row_high[own], row_low[own]], axis=0)
        prod = dot(left, jnp.concatenate([g[s], m[s]], axis=1))
        picked.append(prod[:64] + prod[64:])
    left = jnp.concatenate(picked, axis=0)
    return split(jnp.concatenate([left[:, :GROUP], left[:, GROUP:]], axis=0))


def forward_cols(highs, lows, cols, t_right):
    lane = lax.broadcasted_iota(jnp.int32, (FB, GROUP), 1) // FB
    lhs = jnp.concatenate([jnp.concatenate(highs, axis=0), jnp.concatenate(lows, axis=0)], axis=1)
    prod = dot(lhs, t_right[...])
    prod = prod[:, :GROUP] + prod[:, GROUP:]
    result = []
    for k, col in enumerate(cols):
        tiles = []
        for at in (2 * k * GROUP, (2 * k + 1) * GROUP):
            tile = None
            for q in range(8):
                shift = lax.bitwise_and(FB * q - lax.shift_left(col[q], 4), GROUP - 1)
                part = pltpu.roll(prod[at + FB * q : at + FB * q + FB], shift, 1)
                tile = part if q == 0 else jnp.where(lane == q, part, tile)
            tiles.append(tile)
        result.append(tiles)
    return result


def forward_kernel(swapped, sel_in, g, m, t_high, t_low, t_right, cg, cm, g_buf, m_buf, sel, sem, sel_sem):
    base = half_base(swapped)
    picked = pltpu.make_async_copy(sel_in, sel, sel_sem)
    picked.start()
    wait = load_half((g, m), (g_buf, m_buf), sem, base)
    picked.wait()

    def body(i, _):
        highs, lows = [], []
        for u in range(UNROLL):
            p = i * UNROLL + u
            if u % STEP == 0:
                wait(i * (UNROLL // STEP) + u // STEP)
            pair = pl.ds(2 * p, 2)
            high, low = forward_rows(g_buf[pair], m_buf[pair], rows_of(sel, base + p), t_high, t_low)
            highs.append(high)
            lows.append(low)
        for u in range(0, UNROLL, 2):
            p = i * UNROLL + u
            cols = [cols_of(sel, base + p + k) for k in range(2)]
            tiles = forward_cols(highs[u : u + 2], lows[u : u + 2], cols, t_right)
            for k in range(2):
                cg[p + k], cm[p + k] = tiles[k]
        return 0

    lax.fori_loop(0, HALF // UNROLL, body, 0)


def forward(sel, swapped, grads, momentum, *tables):
    shape = jax.ShapeDtypeStruct((HALF, FB, GROUP), jnp.float32)
    buf = pltpu.VMEM((2 * HALF, GROUP, GROUP), jnp.bfloat16)
    return pl.pallas_call(
        functools.partial(forward_kernel, swapped),
        in_specs=[ANY] * 3 + [VMEM] * 3,
        out_specs=[VMEM, VMEM],
        out_shape=[shape, shape],
        scratch_shapes=[
            buf,
            buf,
            pltpu.SMEM((KSEL, 2 * PAIRS), jnp.int32),
            pltpu.SemaphoreType.DMA((2, CHUNKS)),
            pltpu.SemaphoreType.DMA,
        ],
        compiler_params=pltpu.CompilerParams(vmem_limit_bytes=51 << 20),
        cost_estimate=pl.CostEstimate(flops=2 << 30, bytes_accessed=5 << 20, transcendentals=0),
        name="forward_cosine",
    )(sel, grads, momentum, *tables)


def clip_of(first, second):
    square_sum = jnp.sum(first + second)
    entry_count = float(4 * 2 * PAIRS * GROUP * GROUP)
    return jnp.minimum(1.0, lax.rsqrt(jnp.full((1, GROUP), square_sum) / entry_count))


def combine_kernel(first, second, g_other, m_other, g_own, m_own, c_other, c_own, clip):
    clip[...] = clip_of(first[...], second[...])
    scale = clip[...].reshape(1, 1, GROUP)
    c_other[...] = momentum_retention * m_other[...] + scale * g_other[...]
    c_own[...] = momentum_retention * m_own[...] + scale * g_own[...]


def combine(first, second, *tiles):
    shape = jax.ShapeDtypeStruct((HALF, FB, GROUP), jnp.float32)
    return pl.pallas_call(
        combine_kernel,
        in_specs=[VMEM] * 6,
        out_specs=[VMEM] * 3,
        out_shape=[shape, shape, jax.ShapeDtypeStruct((1, GROUP), jnp.float32)],
        input_output_aliases={2: 0, 4: 1},
        compiler_params=pltpu.CompilerParams(vmem_limit_bytes=8 << 20),
        cost_estimate=pl.CostEstimate(flops=1 << 20, bytes_accessed=1 << 20, transcendentals=0),
        name="combine",
    )(first, second, *tiles)


def place_blocks(coeffs, row_of):
    row_of = jnp.broadcast_to(row_of, coeffs.shape)
    high = coeffs.astype(jnp.bfloat16).astype(jnp.float32)
    placed = []
    for part in (high, coeffs - high):
        parts = [jnp.where(row_of == b, part, 0.0) for b in range(NBS)]
        placed.append(jnp.concatenate(parts, axis=0).astype(jnp.bfloat16))
    return placed


def decode_rows(first, second, t_left):
    high = jnp.concatenate([first[0], second[0]], axis=1)
    low = jnp.concatenate([first[1], second[1]], axis=1)
    left = dot(t_left[...], jnp.concatenate([high, low, high], axis=0))
    return split(left[:, :GROUP]), split(left[:, GROUP:])


def decode_cols(high, low, cols, t_high, t_low):
    none = jnp.zeros((64, GROUP), jnp.bfloat16)

    def both(table):
        chosen = gather_rows(table, cols)
        return jnp.concatenate(
            [
                jnp.concatenate([chosen[:64], none], axis=1),
                jnp.concatenate([none, chosen[64:]], axis=1),
            ],
            axis=0,
        )

    col_high, col_low = both(t_high), both(t_low)
    result = dot(
        jnp.concatenate([high, low, high], axis=1),
        jnp.concatenate([col_high, col_high, col_low], axis=0),
    )
    return result[:, :GROUP], result[:, GROUP:]


def decode_kernel(count, swapped, sel_in, *refs):
    arrays, refs = refs[:count], refs[count:]
    scale, coeffs, row_of, t_high, t_low, t_left = refs[:6]
    out = refs[-(count + 8)]
    bufs = refs[-(count + 7) : -7]
    out_buf, high_buf, low_buf, sel, sem, out_sem, sel_sem = refs[-7:]
    base = half_base(swapped)
    picked = pltpu.make_async_copy(sel_in, sel, sel_sem)
    picked.start()
    wait = load_half(arrays, bufs, sem, base)

    def store(c):
        return pltpu.make_async_copy(
            out_buf.at[pl.ds(c * CHUNK_GROUPS, CHUNK_GROUPS)],
            out.at[pl.ds(2 * base + c * CHUNK_GROUPS, CHUNK_GROUPS)],
            out_sem.at[c],
        )

    def first(i, _):
        for u in range(0, UNROLL, 2):
            p = i * UNROLL + u
            placed = [place_blocks(coeffs[p + k], row_of[pl.ds(base + p + k, 1)]) for k in range(2)]
            for k, (high, low) in enumerate(decode_rows(*placed, t_left)):
                high_buf[p + k], low_buf[p + k] = high, low
        return 0

    def second(i, _):
        chunks = UNROLL // STEP
        for k in range(chunks):
            wait(i * chunks + k)
        for u in range(UNROLL):
            p = i * UNROLL + u
            cols = cols_of(sel, base + p)
            for s, taken in enumerate(decode_cols(high_buf[p], low_buf[p], cols, t_high, t_low)):
                wide = bufs[0][2 * p + s].astype(jnp.float32)
                if count == 2:
                    wide = momentum_retention * bufs[1][2 * p + s].astype(jnp.float32) + scale[...] * wide
                out_buf[2 * p + s] = (wide - taken).astype(jnp.bfloat16)
            if (u + 1) % STEP == 0:
                store(i * chunks + u // STEP).start()
        return 0

    lax.fori_loop(0, HALF // UNROLL, first, 0)
    picked.wait()
    lax.fori_loop(0, HALF // UNROLL, second, 0)
    for c in range(CHUNKS):
        store(c).wait()


def decode_half(sel, swapped, arrays, scale, coeffs, row_of, tables, before, name):
    operands = (sel, *arrays, scale, coeffs, row_of, *tables)
    specs = [ANY] + [ANY] * len(arrays) + [VMEM] * 6
    aliases = {}
    if before is not None:
        aliases = {len(operands): 0}
        operands += (before,)
        specs.append(ANY)
    buf = pltpu.VMEM((2 * HALF, GROUP, GROUP), jnp.bfloat16)
    return pl.pallas_call(
        functools.partial(decode_kernel, len(arrays), swapped),
        in_specs=specs,
        out_specs=ANY,
        out_shape=jax.ShapeDtypeStruct((2 * PAIRS, GROUP, GROUP), jnp.bfloat16),
        scratch_shapes=[buf] * (len(arrays) + 1)
        + [pltpu.VMEM((HALF, GROUP, GROUP), jnp.bfloat16)] * 2
        + [
            pltpu.SMEM((2 * PAIRS * KSEL,), jnp.int32),
            pltpu.SemaphoreType.DMA((len(arrays), CHUNKS)),
            pltpu.SemaphoreType.DMA((CHUNKS,)),
            pltpu.SemaphoreType.DMA,
        ],
        input_output_aliases=aliases,
        compiler_params=pltpu.CompilerParams(vmem_limit_bytes=51 << 20),
        cost_estimate=pl.CostEstimate(flops=2 << 30, bytes_accessed=(2 << 20) * (1 + len(arrays)), transcendentals=0),
        name=name,
    )(*operands)


def total_kernel(parts, out):
    total = jnp.sum(parts[...], axis=0)
    lane = lax.broadcasted_iota(jnp.int32, (FB, GROUP), 1)
    square = total * total
    square = jnp.sum(square, axis=0, keepdims=True)
    lane = lane[:1]
    first = jnp.sum(jnp.where(lane < 64, square, 0.0), axis=1, keepdims=True)
    second = jnp.sum(jnp.where(lane < 64, 0.0, square), axis=1, keepdims=True)
    mean = jnp.where(lane < 64, first, second) / (GROUP * GROUP)
    out[...] = jnp.broadcast_to(learn_rate * total * lax.rsqrt(mean + eps), out.shape)


def scaled_totals(parts):
    return pl.pallas_call(
        total_kernel,
        in_specs=[VMEM],
        out_specs=VMEM,
        out_shape=jax.ShapeDtypeStruct((CHIPS, FB, GROUP), jnp.float32),
        compiler_params=pltpu.CompilerParams(vmem_limit_bytes=8 << 20),
        cost_estimate=pl.CostEstimate(flops=1 << 20, bytes_accessed=1 << 19, transcendentals=0),
        name="scaled_totals",
    )(parts)


def per_device(grads, momentum, weight, select):
    high, low = dct_tables()
    left = np.concatenate([high.T, high.T, low.T], axis=1)
    right = np.concatenate([high.T, low.T, high.T, np.zeros_like(low)], axis=1)
    t_right = jnp.asarray(np.concatenate([right[:, : 2 * GROUP], right[:, 2 * GROUP :]], axis=0))
    t_high, t_low, t_left = tables = tuple(jnp.asarray(table) for table in (high, low, left))
    grads, momentum = grads[0], momentum[0]
    same_core = [[(c + 2 * (18 + k)) % REPS for k in range(CHIPS)] for c in range(2)]
    swap_core = [(i, i ^ 1) for i in range(REPS)]
    swap = lambda x: lax.ppermute(x, "rep", swap_core)
    exchange = lambda x: lax.all_to_all(x, "rep", 0, 0, tiled=True, axis_index_groups=same_core)

    sums = square_sums(grads)
    sums += lax.ppermute(sums, "mdl", [(i, i ^ 1) for i in range(4)])
    g_other, m_other = forward(select.T, True, grads, momentum, t_high, t_low, t_right)
    sums, g_other, m_other = lax.optimization_barrier((sums, g_other, m_other))
    far = lax.ppermute(sums, "mdl", [(i, i ^ 2) for i in range(4)])
    g_own, m_own = forward(select.T, False, grads, momentum, t_high, t_low, t_right)
    c_other, c_own, clip = combine(sums, far, g_other, m_other, g_own, m_own)
    chip, c_other, c_own = lax.optimization_barrier((c_own + swap(c_other), c_other, c_own))
    select, _ = lax.optimization_barrier((select, chip))
    sel = select.reshape(-1)
    row_of = jnp.repeat(lax.shift_right_logical(select, 3), FB, axis=1).reshape(PAIRS, GROUP)
    parts = exchange(chip)
    new_momentum = decode_half(
        sel, True, (grads, momentum), clip, c_other, row_of, tables, None, "momentum_other"
    )
    parts, new_momentum = lax.optimization_barrier((parts, new_momentum))
    mine, c_own = lax.optimization_barrier((scaled_totals(parts), c_own))
    totals_own = exchange(mine)
    new_momentum = decode_half(
        sel, False, (grads, momentum), clip, c_own, row_of, tables, new_momentum, "momentum_own"
    )
    totals_own, new_momentum = lax.optimization_barrier((totals_own, new_momentum))
    totals_other = swap(totals_own)
    new_weight = decode_half(sel, False, (weight,), clip, totals_own, row_of, tables, None, "weight_own")
    new_weight = decode_half(
        sel, True, (weight,), clip, totals_other, row_of, tables, new_weight, "weight_other"
    )
    return (new_weight, new_momentum[None])


def solution(mesh):
    return jax.shard_map(
        per_device,
        mesh=mesh,
        in_specs=(
            P("rep", "mdl", None, None),
            P("rep", "mdl", None, None),
            P("mdl", None, None),
            P("mdl", None),
        ),
        out_specs=(P("mdl", None, None), P("rep", "mdl", None, None)),
        check_vma=False,
    )
```
